128 devices in a mesh: section: 8 (over x_hi, y), feat: 16 (over x_lo, z, core).
Axes of the slice: x: 4 (x_hi: 2, x_lo: 2; x = x_hi * 2 + x_lo), y: 4, z: 4, core: 2. Of those that a mesh axis runs over, the one named last changes fastest.
Arguments:
- resid_in: bfloat16 [1024, 8192], P('feat', 'section'), may hold values from -6 to 6
- active: int32 [1024, 24], replicated, may hold values from 0 to 255, all different within a row; in each aligned block of 64 rows (0 to 63, 64 to 127, ...) at most 24 rows name the same one
- enc_weight: bfloat16 [8192, 32768], P('section', 'feat'), may hold values from -0.0625 to 0.0625
- enc_bias: float32 [32768], P('feat'), may hold values from -3 to 3
- dec_weight: bfloat16 [8, 32768, 4096], P('section', 'feat'), may hold values from -0.109375 to 0.109375
- target_resid: bfloat16 [8, 1024, 4096], P('section', 'feat'), may hold values from -6 to 6
- slot_block: int32 [256], replicated, may hold values from 0 to 255, each once
- source: int32 [1024], P('feat'), may hold values from 0 to 7
Outputs:
- recon_error: bfloat16 [8, 1024, 4096], P('section', 'feat')
The draws below stay inside these ranges and needn't reach their ends.
Inputs may be any that keep to these rules, and one draw needn't show every extreme that they name: `active`: each token names 24 different blocks. Among the 64 tokens of one feat index (aligned blocks of 64 rows) no block is named by more than 24 tokens, and some block by exactly 24. `slot_block`: every block number appears once.
All inputs are finite; a program needn't handle non-finite values.
Results may differ from the reference program's by a relative error of at most 0.019.
Values may be sent and summed in bfloat16 or wider, within the bound.
No kernel may reach another device: no remote copies, remote signals or barrier semaphores. Data moves between devices by JAX's collectives and lax.ppermute only.
A program may use at most 128 MiB of HBM per device.

```python
import math
import jax
import jax.numpy as jnp
import numpy as np
from jax import lax

D = 8192
DW = 4096
F = 32768
BLK = 128
K = 24
M = 24
TOK_DEV = 64
NB = 256
BPO = 16
CAPB = 384
TOKENS = 1024
N_SECTION = 8
N_FEAT = 16


def with_ends(values, key, smallest, high):
    spot = [jax.random.randint(jax.random.fold_in(key, axis), (), 0, length) for axis, length in enumerate(values.shape)]
    longest = values.shape.index(max(values.shape))
    beside = spot[:longest] + [(spot[longest] + 1) % values.shape[longest]] + spot[longest + 1:]
    return values.at[tuple(spot)].set(smallest).at[tuple(beside)].set(high)


def levels(own_key, extent, split, smallest, high):
    loudness = 1.0
    for axis_at, parts in split:
        draws = jax.random.uniform(jax.random.fold_in(jax.random.fold_in(own_key, 6), axis_at), (parts,), jnp.float32, smallest / len(split), high / len(split))
        loudness = loudness * jnp.repeat(jnp.exp(draws), extent[axis_at] // parts).reshape((-1,) + (1,) * (len(extent) - 1 - axis_at))
    return loudness


def deal_out(key, own, number, rows, amount, top, reach, slope):
    sequence = jax.random.permutation(key, amount)
    crowded, usual = load_shares(amount, rows * top, reach, slope, True), load_shares(amount, rows * top, reach, slope, False)
    places = jnp.arange(amount)

    def named(sizes, offset_by):
        used = int((sizes > 0).sum())
        fixed = max(1, used // 4)
        shifted = fixed + (places - fixed + offset_by * (used - fixed)) % max(1, amount - fixed)
        return jnp.zeros((amount,), jnp.int32).at[sequence[jnp.where(places < fixed, places, shifted)]].set(jnp.asarray(sizes, jnp.int32))

    sizes = jnp.where(number % 4 == 0, named(crowded, number // 4), named(usual, number - number // 4 - 1))
    mixed = jax.random.permutation(jax.random.fold_in(own, 3), amount)
    giver, taker = mixed[0:amount // 2 * 2:2], mixed[1:amount // 2 * 2:2]
    margin = jnp.minimum(sizes[giver] - 1, reach - sizes[taker]) // 2
    margin = jnp.where((giver == sequence[0]) | (taker == sequence[0]) | (sizes[taker] == 0), 0, jnp.maximum(margin, 0))
    shifted = jax.random.randint(jax.random.fold_in(own, 4), (amount // 2,), 0, 1 << 20) % (margin + 1)
    sizes = sizes.at[giver].add(-shifted).at[taker].add(shifted)
    labels = jnp.searchsorted(jnp.cumsum(sizes), jnp.arange(rows * top), side="right").astype(jnp.int32)
    table = labels.reshape(top, rows).T
    table = table[jax.random.permutation(jax.random.fold_in(own, 1), rows)]
    offset_by = jax.random.randint(jax.random.fold_in(own, 2), (rows, 1), 0, top)
    return jnp.take_along_axis(table, (jnp.arange(top)[None, :] + offset_by) % top, axis=1)


def load_shares(count, total, bound, slope, full):
    weights = [(1 << 20) // math.isqrt(standing ** slope) + 1 for standing in range(1, count + 1)]
    largest = bound if full else min(bound, max(-(-total // count), total * weights[0] // sum(weights)))
    least = 1 if total - largest >= count - 1 else 0
    counts, spare = [largest] + [least] * (count - 1), total - largest - least * (count - 1)
    while spare > 0:
        movable = [i for i in range(1, count) if counts[i] < largest] or [i for i in range(1, count) if counts[i] < bound]
        pool, left = sum([weights[i] for i in movable]), spare
        for i in movable:
            more = min(bound - counts[i], max(1, left * weights[i] // pool), spare)
            counts[i] = counts[i] + more
            spare = spare - more
    return np.array(counts)


def gaussian(key, shape, scale, limit, cuts=(), kind=jnp.bfloat16):
    gain = levels(key, shape, cuts, -0.22, 0.18) if cuts else 1.0
    entries = jax.random.normal(key, shape, jnp.float32) * scale * gain
    return jnp.minimum(jnp.maximum(entries, -limit), limit).astype(kind)


def setup_inputs(seed: int = 0) -> dict:
    key_of = jax.random.split(jax.random.key(seed), 9)
    resid_in = gaussian(key_of[0], (TOKENS, D), 1.0, 6.0, ((0, 16), (1, 8)))
    active_keys = jax.random.split(jax.random.fold_in(key_of[1], 1), TOKENS // TOK_DEV)
    active_turns = jax.random.permutation(jax.random.fold_in(key_of[1], 3), TOKENS // TOK_DEV)
    active = jax.vmap(lambda own, number: deal_out(jax.random.fold_in(key_of[1], 2), own, number, TOK_DEV, NB, K, M, 2))(active_keys, active_turns).reshape((TOKENS, K))
    enc_weight = gaussian(key_of[2], (D, F), D ** -0.5, 0.0625, ((0, 8), (1, 16)))
    enc_bias = gaussian(key_of[3], (F,), 0.5, 3.0, ((0, 16),), jnp.float32)
    dec_weight = gaussian(key_of[4], (N_SECTION, F, DW), (K * BLK) ** -0.5, 0.109375, ((0, 8), (1, 16)))
    target_resid = gaussian(key_of[5], (N_SECTION, TOKENS, DW), 1.0, 6.0, ((0, 8), (1, 16)))
    slot_block = jax.random.permutation(key_of[6], NB).astype(jnp.int32)
    source = with_ends(jax.random.randint(key_of[7], (TOKENS,), 0, N_SECTION), jax.random.fold_in(key_of[7], 1), 0, N_SECTION - 1).astype(jnp.int32)
    return {"resid_in": resid_in, "active": active, "enc_weight": enc_weight, "enc_bias": enc_bias, "dec_weight": dec_weight, "target_resid": target_resid, "slot_block": slot_block, "source": source}


def reference(resid_in, active, enc_weight, enc_bias, dec_weight, target_resid, slot_block, source):
    padded = jnp.concatenate([resid_in, jnp.zeros((1, D), resid_in.dtype)], axis=0)

    def owner_part(owner_index):
        def advance(totals, position):
            storage = (owner_index * BPO + position).astype(jnp.int32)
            block_id = slot_block[storage]
            matched = jnp.any(active == block_id, axis=1)
            index_list = jnp.nonzero(matched, size=CAPB, fill_value=TOKENS)[0].astype(jnp.int32)
            selected = padded[index_list]
            enc_block = lax.dynamic_slice_in_dim(enc_weight, storage * BLK, BLK, 1)
            bias_block = lax.dynamic_slice_in_dim(enc_bias, storage * BLK, BLK, 0)
            preact = jnp.dot(selected, enc_block, preferred_element_type=jnp.float32) + bias_block
            activation = jnp.where((index_list < TOKENS)[:, None], jax.nn.relu(preact), jnp.float32(0.0)).astype(jnp.bfloat16)
            dec_block = lax.dynamic_slice_in_dim(dec_weight, storage * BLK, BLK, 1)
            decoded = jnp.einsum("ck,skw->csw", activation.astype(jnp.float32), dec_block.astype(jnp.float32))
            return totals.at[index_list].add(decoded), None

        start = jnp.zeros((TOKENS + 1, N_SECTION, DW), jnp.float32)
        totals, unused = lax.scan(advance, start, jnp.arange(BPO, dtype=jnp.int32))
        return totals[:TOKENS].astype(jnp.bfloat16)

    def add_owner(recon, owner_index):
        return recon + owner_part(owner_index).astype(jnp.float32), None

    recon, unused = lax.scan(add_owner, jnp.zeros((TOKENS, N_SECTION, DW), jnp.float32), jnp.arange(N_FEAT, dtype=jnp.int32))
    recon = jnp.transpose(recon, (1, 0, 2))
    target = target_resid.astype(jnp.float32)
    keep_mask = (jnp.arange(N_SECTION, dtype=jnp.int32)[:, None] >= source[None, :])[:, :, None]
    return jnp.where(keep_mask, target - recon, target).astype(jnp.bfloat16)
```

```python
import functools

import jax
import jax.numpy as jnp
from jax import lax
from jax.experimental import pallas as pl
from jax.experimental.pallas import tpu as pltpu
from jax.sharding import PartitionSpec as P

BLK = 128
GRP = 64
CAP = 384
TOK = 1024
NPOS = 256
OWN = 16
FULL = OWN * CAP
SMALL = FULL // 2
WIN = 128
HALF = 512
XL, Z, C = 2, 4, 2
BF = jnp.bfloat16
F32 = jnp.float32
I32 = jnp.int32
VM = pl.BlockSpec(memory_space=pltpu.VMEM)
SM = pl.BlockSpec(memory_space=pltpu.SMEM)
ANY = pl.BlockSpec(memory_space=pl.ANY)


def feat_perm(move):
    pairs = []
    for xl in range(XL):
        for z in range(Z):
            for c in range(C):
                a, b, d = move(xl, z, c)
                pairs.append(((xl * Z + z) * C + c, (a * Z + b) * C + d))
    return pairs


UP = feat_perm(lambda xl, z, c: (xl, (z + 1) % Z, c))
DOWN = feat_perm(lambda xl, z, c: (xl, (z + Z - 1) % Z, c))
SWAP_X = feat_perm(lambda xl, z, c: (1 - xl, z, c))
SWAP_C = feat_perm(lambda xl, z, c: (xl, z, 1 - c))
SAME_C = [[(xl * Z + z) * C + c for xl in range(XL) for z in range(Z)] for c in range(C)]


def move(x, pairs):
    return lax.ppermute(x, "feat", pairs)


def iota(shape, dim):
    return lax.broadcasted_iota(I32, shape, dim)


def index_kernel(where_ref, active_ref, slot_ref, rows_ref, cols_ref, meta_ref, most_ref, act, rowt):
    f = where_ref[0]
    xl, z, c = f // (Z * C), (f // C) % Z, f % C
    for cc in range(C):
        for xr in range(XL):
            for zr in range(Z):
                g = ((xl + xr) % XL * Z + (z + zr) % Z) * C + cc
                to = ((cc * XL + xr) * Z + zr) * GRP
                act[to : to + GRP, :] = active_ref[pl.ds(pl.multiple_of(g * GRP, GRP), GRP), :]
    slots = slot_ref[...]
    parts = []
    for r in range(0, TOK, 128):
        rows = act[r : r + 128, :]
        hit = rows[:, 0:1] == slots
        for k in range(1, rows.shape[1]):
            hit = jnp.logical_or(hit, rows[:, k : k + 1] == slots)
        parts.append(jnp.where(hit, 1.0, 0.0).astype(BF))
    hits = jnp.concatenate(parts, axis=0)
    lane = iota((NPOS, 128), 1)
    other = f + 1 - 2 * c
    wanted = jnp.where(lane < OWN, f * OWN + lane, other * OWN + lane - OWN)
    pick = jnp.where((iota((NPOS, 128), 0) == wanted) & (lane < 2 * OWN), 1.0, 0.0).astype(BF)
    mine = jnp.dot(hits, pick, preferred_element_type=F32).astype(BF)
    lower = jnp.where(iota((TOK, TOK), 0) > iota((TOK, TOK), 1), 1.0, 0.0).astype(BF)
    before = jnp.dot(lower, mine, preferred_element_type=F32)
    ones = jnp.ones((8, TOK), BF)
    every = jnp.dot(ones, hits, preferred_element_type=F32)
    counts = jnp.dot(ones, mine, preferred_element_type=F32)
    units = jnp.floor((counts + 15.0) * (1.0 / 16.0))
    i, j = iota((128, 128), 0), iota((128, 128), 1)
    chain = jnp.where((i < j) & (i // OWN == j // OWN), 1.0, 0.0).astype(BF)
    starts = jnp.dot(units.astype(BF), chain, preferred_element_type=F32) * 16.0
    group = jnp.where(iota((NPOS, 128), 0) // OWN == lane, 1.0, 0.0).astype(BF)
    every_units = jnp.floor((every + 15.0) * (1.0 / 16.0)).astype(BF)
    totals = jnp.dot(every_units, group, preferred_element_type=F32) * 16.0
    most_ref[0, 0] = jnp.max(totals).astype(I32)
    meta_ref[0:8, :] = starts.astype(I32)
    meta_ref[8:16, :] = counts.astype(I32)
    placed = jnp.where(mine > 0.5, before + starts[0:1, :], -1.0)
    rowt[...] = placed
    cols_ref[...] = rowt[pl.ds(pl.multiple_of(c * HALF, HALF), HALF), :].astype(I32)
    rows_ref[...] = jnp.transpose(placed)[: 2 * OWN, :].astype(I32)


def index_call(where, active, slots):
    return pl.pallas_call(
        index_kernel,
        in_specs=[SM, VM, VM],
        out_specs=[VM, VM, VM, SM],
        out_shape=[
            jax.ShapeDtypeStruct((2 * OWN, TOK), I32),
            jax.ShapeDtypeStruct((HALF, 128), I32),
            jax.ShapeDtypeStruct((16, 128), I32),
            jax.ShapeDtypeStruct((1, 1), I32),
        ],
        scratch_shapes=[pltpu.VMEM((TOK, active.shape[1]), I32), pltpu.VMEM((TOK, 128), F32)],
        compiler_params=pltpu.CompilerParams(vmem_limit_bytes=32 << 20),
        cost_estimate=pl.CostEstimate(flops=4 << 30, bytes_accessed=1 << 20, transcendentals=0),
    )(where, active, slots)


def encode_kernel(where_ref, meta_ref, near_ref, far_ref, rows_ref, enc_ref, out_ref, tok, sems):
    step = pl.program_id(0)

    @pl.when(step == 0)
    def _():
        f = where_ref[0]
        xl, z, c = f // (Z * C), (f // C) % Z, f % C
        copies = []
        for side, (src, core) in enumerate(((near_ref, c), (far_ref, 1 - c))):
            for xr in range(XL):
                for zr in range(Z):
                    g = (xl + xr) % XL * Z + (z + zr) % Z
                    to = pl.multiple_of(core * HALF + (xr * Z + zr) * GRP, GRP)
                    copies.append(
                        pltpu.make_async_copy(
                            src.at[g], tok.at[pl.ds(to, GRP), :], sems.at[side * 8 + xr * Z + zr]
                        )
                    )
        for copy in copies:
            copy.start()
        for copy in copies:
            copy.wait()

    y = jnp.dot(tok[...], enc_ref[...], preferred_element_type=F32).astype(BF)
    for b in range(2):
        block = step * 2 + b
        start, count = meta_ref[0, block], meta_ref[8, block]
        yb = y[:, b * BLK : (b + 1) * BLK]
        place = rows_ref[pl.ds(block, 1), :]
        for w in range(CAP // WIN):
            at = pl.multiple_of(start + w * WIN, 16)

            @pl.when((count > w * WIN) | (w == 0))
            def _(at=at):
                one = jnp.where(iota((WIN, TOK), 0) + at == place, 1.0, 0.0).astype(BF)
                out_ref[pl.ds(at, WIN), :] = jnp.dot(one, yb, preferred_element_type=F32).astype(BF)


def encode_call(where, meta, near, far, rows, enc):
    return pl.pallas_call(
        encode_kernel,
        grid=(OWN // 2,),
        in_specs=[
            SM,
            SM,
            ANY,
            ANY,
            pl.BlockSpec((2 * OWN, TOK), lambda i: (0, 0)),
            pl.BlockSpec((enc.shape[0], 2 * BLK), lambda i: (0, i)),
        ],
        out_specs=pl.BlockSpec((FULL, BLK), lambda i: (0, 0)),
        out_shape=jax.ShapeDtypeStruct((FULL, BLK), BF),
        scratch_shapes=[pltpu.VMEM((TOK, enc.shape[0]), BF), pltpu.SemaphoreType.DMA((16,))],
        compiler_params=pltpu.CompilerParams(
            vmem_limit_bytes=32 << 20, dimension_semantics=("arbitrary",)
        ),
        cost_estimate=pl.CostEstimate(flops=6 << 30, bytes_accessed=8 << 20, transcendentals=0),
    )(where, meta, near, far, rows, enc)


def reduce_kernel(where_ref, meta_ref, parts_ref, bias_ref, out_ref):
    share = out_ref.shape[0]
    total = parts_ref[0].astype(F32)
    for s in range(1, parts_ref.shape[0]):
        total = total + parts_ref[s].astype(F32)
    row = iota((share, BLK), 0) + where_ref[1] * share
    bias = jnp.zeros((share, BLK), F32)
    for b in range(OWN):
        bias = jnp.where(row >= meta_ref[0, b], bias_ref[b : b + 1, :], bias)
    last = meta_ref[0, OWN - 1] + meta_ref[8, OWN - 1]
    out_ref[...] = jnp.where(row < last, jnp.maximum(total + bias, 0.0), 0.0).astype(BF)


def reduce_call(where, meta, parts, bias):
    return pl.pallas_call(
        reduce_kernel,
        in_specs=[SM, SM, VM, VM],
        out_specs=VM,
        out_shape=jax.ShapeDtypeStruct(parts.shape[1:], BF),
        compiler_params=pltpu.CompilerParams(vmem_limit_bytes=32 << 20),
        cost_estimate=pl.CostEstimate(flops=16 << 20, bytes_accessed=4 << 20, transcendentals=0),
    )(where, meta, parts, bias)


def spread_kernel(first, meta_ref, cols_ref, act_ref, out_ref):
    rows = act_ref.shape[0]
    cols = cols_ref[...]
    for b in range(OWN):
        start, count = meta_ref[0, first + b], meta_ref[8, first + b]
        place = cols[:, first + b : first + b + 1]

        def window(w, start=start, place=place):
            begin = start + w * WIN
            at = pl.multiple_of(jnp.minimum(begin, rows - WIN), 16)
            spot = iota((HALF, WIN), 1) + at
            one = jnp.where((spot == place) & (spot >= begin), 1.0, 0.0).astype(BF)
            return jnp.dot(one, act_ref[pl.ds(at, WIN), :], preferred_element_type=F32).astype(BF)

        out_ref[:, b * BLK : (b + 1) * BLK] = window(0)
        for w in range(1, CAP // WIN):

            @pl.when(count > w * WIN)
            def _(w=w, b=b, window=window):
                out_ref[:, b * BLK : (b + 1) * BLK] += window(w)


def spread_call(first, meta, cols, act):
    return pl.pallas_call(
        functools.partial(spread_kernel, first),
        in_specs=[SM, VM, VM],
        out_specs=VM,
        out_shape=jax.ShapeDtypeStruct((HALF, OWN * BLK), BF),
        compiler_params=pltpu.CompilerParams(vmem_limit_bytes=32 << 20),
        cost_estimate=pl.CostEstimate(flops=1 << 30, bytes_accessed=4 << 20, transcendentals=0),
    )(meta, cols, act)


def decode_kernel(kind, half, a1_ref, a2_ref, w1_ref, w2_ref, after_ref, *outs):
    y = jnp.dot(a1_ref[...], w1_ref[...], preferred_element_type=F32)
    y = y + jnp.dot(a2_ref[...], w2_ref[...], preferred_element_type=F32)
    y = y.astype(BF)
    if kind == "x":
        outs[0][...] = y[: HALF // 2]
        outs[1][...] = y[HALF // 2 :]
        return
    z2 = []
    for zr, out in ((0, outs[0]), (1, outs[1]), (3, outs[2])):
        out[0:GRP, :] = y[zr * GRP : (zr + 1) * GRP]
        out[GRP : 2 * GRP, :] = y[HALF // 2 + zr * GRP : HALF // 2 + (zr + 1) * GRP]
    step = pl.program_id(0)
    for out, here in ((outs[3], step < half), (outs[4], step >= half)):

        @pl.when(here)
        def _(out=out):
            out[0:GRP, :] = y[2 * GRP : 3 * GRP]
            out[GRP : 2 * GRP, :] = y[HALF // 2 + 2 * GRP : HALF // 2 + 3 * GRP]


def decode_call(kind, a1, a2, w1, w2, first, width, after, tile=512):
    steps, base = width // tile, first // tile
    half = steps // 2
    depth = w1.shape[0]
    weights = pl.BlockSpec((depth, tile), lambda i: (0, base + i))
    acts = pl.BlockSpec((HALF, depth), lambda i: (0, 0))
    if kind == "x":
        shapes = [(HALF // 2, width)] * 2
        specs = [pl.BlockSpec((HALF // 2, tile), lambda i: (0, i))] * 2
    else:
        shapes = [(2 * GRP, width)] * 3 + [(2 * GRP, half * tile), (2 * GRP, width - half * tile)]
        specs = [pl.BlockSpec((2 * GRP, tile), lambda i: (0, i))] * 3 + [
            pl.BlockSpec((2 * GRP, tile), lambda i: (0, jnp.minimum(i, half - 1))),
            pl.BlockSpec((2 * GRP, tile), lambda i: (0, jnp.maximum(i - half, 0))),
        ]
    return pl.pallas_call(
        functools.partial(decode_kernel, kind, half),
        grid=(steps,),
        in_specs=[acts, acts, weights, weights, ANY],
        out_specs=specs,
        out_shape=[jax.ShapeDtypeStruct(s, BF) for s in shapes],
        compiler_params=pltpu.CompilerParams(
            vmem_limit_bytes=40 << 20, dimension_semantics=("arbitrary",)
        ),
        cost_estimate=pl.CostEstimate(
            flops=4 * HALF * depth * width,
            bytes_accessed=4 * depth * width + HALF * width * 2 + 4 * HALF * depth,
            transcendentals=0,
        ),
    )(a1, a2, w1, w2, after)


def add(*terms):
    total = terms[0].astype(F32)
    for term in terms[1:]:
        total = total + term.astype(F32)
    return total


def ring_sum(z0, z1, z3, left, right):
    h = left.shape[1]
    got_left, got_right = move(left, UP), move(right, DOWN)
    up = jnp.concatenate([add(z1[:, :h], got_left).astype(BF), z1[:, h:]], axis=1)
    down = jnp.concatenate([z3[:, :h], add(z3[:, h:], got_right).astype(BF)], axis=1)
    return add(z0, move(up, UP), move(down, DOWN))


PLAN = (("x", 2048), ("z", 2048))


def body(resid_in, active, enc_weight, enc_bias, dec_weight, target_resid, slot_block, source):
    feat_index = lax.axis_index("feat")
    section_index = lax.axis_index("section")
    sections = lax.axis_size("section")
    where = jnp.stack([feat_index, section_index]).astype(I32)
    decoder = dec_weight[0]
    other_decoder = move(decoder, SWAP_C)
    rows, cols, meta, most = index_call(where, active, slot_block.reshape(1, NPOS))
    copies = jnp.broadcast_to(resid_in[None], (XL * Z,) + resid_in.shape)
    near = lax.all_to_all(copies, "feat", 0, 0, axis_index_groups=SAME_C)
    far = move(near, SWAP_C)
    packed = encode_call(where, meta, near, far, rows, enc_weight)
    bias = enc_bias.reshape(OWN, BLK)

    def exchange(room, packed):
        share = room // sections
        parts = packed[:room].reshape(sections, share, BLK)
        parts = lax.all_to_all(parts, "section", 0, 0)
        mine = reduce_call(where, meta, parts, bias)
        wide = jnp.broadcast_to(mine[None], (sections, share, BLK))
        act = lax.all_to_all(wide, "section", 0, 0).reshape(room, BLK)
        other = move(act, SWAP_C)
        return spread_call(0, meta, cols, act), spread_call(OWN, meta, cols, other)

    own, theirs = lax.cond(
        most[0, 0] <= SMALL,
        functools.partial(exchange, SMALL),
        functools.partial(exchange, FULL),
        packed,
    )

    pieces, first, after = [], 0, meta
    for kind, width in PLAN:
        outs = decode_call(kind, own, theirs, decoder, other_decoder, first, width, after)
        pieces.append((kind, width, outs))
        first, after = first + width, outs[0]
    recon = []
    for kind, width, outs in pieces:
        if kind == "x":
            stay, leave = outs
            total = add(stay, move(leave, SWAP_X)).astype(BF).reshape(Z, GRP, width)
            h = width // 2
            recon.append(ring_sum(total[0], total[1], total[3], total[2][:, :h], total[2][:, h:]))
        else:
            total = ring_sum(*outs)
            recon.append(add(total[:GRP], move(total[GRP:].astype(BF), SWAP_X)))
    recon = jnp.concatenate(recon, axis=1)
    target = target_resid[0].astype(F32)
    keep_mask = section_index >= source[:, None]
    result = jnp.where(keep_mask, target - recon, target).astype(BF)
    return result[None]


def solution(mesh):
    placed = (
        P("feat", "section"),
        P(),
        P("section", "feat"),
        P("feat"),
        P("section", "feat", None),
        P("section", "feat", None),
        P(),
        P("feat"),
    )
    return jax.shard_map(
        body, mesh=mesh, in_specs=placed, out_specs=P("section", "feat", None), check_vma=False
    )
```

```python
import functools

import jax
import jax.numpy as jnp
from jax import lax
from jax.experimental import pallas as pl
from jax.experimental.pallas import tpu as pltpu
from jax.sharding import PartitionSpec as P

BLK = 128
GRP = 64
CAP = 384
TOK = 1024
NPOS = 256
OWN = 16
FULL = OWN * CAP
SMALL = FULL // 2
WIN = 128
HALF = 512
XL, Z, C = 2, 4, 2
BF = jnp.bfloat16
F32 = jnp.float32
I32 = jnp.int32
VM = pl.BlockSpec(memory_space=pltpu.VMEM)
SM = pl.BlockSpec(memory_space=pltpu.SMEM)
ANY = pl.BlockSpec(memory_space=pl.ANY)


def feat_perm(move):
    pairs = []
    for xl in range(XL):
        for z in range(Z):
            for c in range(C):
                a, b, d = move(xl, z, c)
                pairs.append(((xl * Z + z) * C + c, (a * Z + b) * C + d))
    return pairs


UP = feat_perm(lambda xl, z, c: (xl, (z + 1) % Z, c))
DOWN = feat_perm(lambda xl, z, c: (xl, (z + Z - 1) % Z, c))
SWAP_X = feat_perm(lambda xl, z, c: (1 - xl, z, c))
SWAP_C = feat_perm(lambda xl, z, c: (xl, z, 1 - c))
SAME_C = [[(xl * Z + z) * C + c for xl in range(XL) for z in range(Z)] for c in range(C)]


def move(x, pairs):
    return lax.ppermute(x, "feat", pairs)


def iota(shape, dim):
    return lax.broadcasted_iota(I32, shape, dim)


def index_kernel(where_ref, active_ref, slot_ref, rows_ref, cols_ref, meta_ref, most_ref, hits, rowt):
    f = where_ref[0]
    xl, z, c = f // (Z * C), (f // C) % Z, f % C
    for p in range(0, NPOS, 32):
        slots = jnp.broadcast_to(slot_ref[p : p + 32, :], (32, 128))
        for t in range(0, TOK, 128):
            named = active_ref[:, t : t + 128]
            hit = named[0:1, :] == slots
            for k in range(1, active_ref.shape[0]):
                hit = jnp.logical_or(hit, named[k : k + 1, :] == slots)
            hits[p : p + 32, t : t + 128] = jnp.where(hit, 1.0, 0.0).astype(BF)
    ones = jnp.ones((TOK, 128), BF)
    every = jnp.dot(hits[...], ones, preferred_element_type=F32)
    group = jnp.where(iota((OWN, NPOS), 1) // OWN == iota((OWN, NPOS), 0), 1.0, 0.0).astype(BF)
    units = jnp.floor((every + 15.0) * (1.0 / 16.0)).astype(BF)
    totals = jnp.dot(group, units, preferred_element_type=F32) * 16.0
    most_ref[0, 0] = jnp.max(totals).astype(I32)
    other = f + 1 - 2 * c
    mine = jnp.concatenate(
        [hits[pl.ds(pl.multiple_of(o * OWN, OWN), OWN), :] for o in (f, other)], axis=0
    )
    tiles = TOK // 128
    stack = jnp.concatenate([mine[:, t * 128 : (t + 1) * 128] for t in range(tiles)], axis=0)
    i, j = iota((128, 128), 0), iota((128, 128), 1)
    inside = jnp.dot(stack, jnp.where(i < j, 1.0, 0.0).astype(BF), preferred_element_type=F32)
    sums = jnp.dot(stack, jnp.ones((128, 128), BF), preferred_element_type=F32)
    n = 2 * OWN
    running = [jnp.zeros((n, 128), F32)]
    for t in range(tiles):
        running.append(running[-1] + sums[t * n : (t + 1) * n])
    counts = running[-1]
    own_units = jnp.floor((counts + 15.0) * (1.0 / 16.0)).astype(BF)
    ci, cj = iota((n, n), 0), iota((n, n), 1)
    chain = jnp.where((cj < ci) & (ci // OWN == cj // OWN), 1.0, 0.0).astype(BF)
    starts = jnp.dot(chain, own_units, preferred_element_type=F32) * 16.0
    placed = [
        jnp.where(
            stack[t * n : (t + 1) * n].astype(F32) > 0.5,
            inside[t * n : (t + 1) * n] + running[t] + starts,
            -1.0,
        )
        for t in range(tiles)
    ]
    low = iota((n, 128), 1) < GRP
    for t in range(tiles // 2):
        even, odd = placed[2 * t], placed[2 * t + 1]
        core0 = jnp.where(low, even, pltpu.roll(odd, GRP, 1))
        core1 = jnp.where(low, pltpu.roll(even, GRP, 1), odd)
        near, far = jnp.where(c == 0, core0, core1), jnp.where(c == 0, core1, core0)
        rows_ref[:, t * 128 : (t + 1) * 128] = near.astype(I32)
        rows_ref[:, HALF + t * 128 : HALF + (t + 1) * 128] = far.astype(I32)
    blank = jnp.full((128 - n, 128), -1.0, F32)
    for t in range(tiles):
        tall = jnp.transpose(jnp.concatenate([placed[t], blank], axis=0))
        rowt[t * 128 : (t + 1) * 128, :] = tall.astype(I32)
    for xr in range(XL):
        for zr in range(Z):
            g = ((xl + xr) % XL * Z + (z + zr) % Z) * C + c
            to = (xr * Z + zr) * GRP
            cols_ref[to : to + GRP, :] = rowt[pl.ds(pl.multiple_of(g * GRP, GRP), GRP), :]
    flat = jnp.transpose(jnp.concatenate([starts, counts, jnp.zeros((64, 128), F32)], axis=0))
    meta_ref[...] = flat[0:8, :].astype(I32)


def index_call(where, active, slots):
    return pl.pallas_call(
        index_kernel,
        in_specs=[SM, VM, VM],
        out_specs=[VM, VM, VM, SM],
        out_shape=[
            jax.ShapeDtypeStruct((2 * OWN, TOK), I32),
            jax.ShapeDtypeStruct((HALF, 128), I32),
            jax.ShapeDtypeStruct((8, 128), I32),
            jax.ShapeDtypeStruct((1, 1), I32),
        ],
        scratch_shapes=[pltpu.VMEM((NPOS, TOK), BF), pltpu.VMEM((TOK, 128), I32)],
        compiler_params=pltpu.CompilerParams(vmem_limit_bytes=32 << 20),
        cost_estimate=pl.CostEstimate(flops=4 << 30, bytes_accessed=1 << 20, transcendentals=0),
    )(where, active, slots)


def encode_kernel(meta_ref, near_ref, far_ref, rows_ref, enc_ref, out_ref, held):
    first = pl.program_id(0) * 2

    def pack(b, w):
        at = pl.multiple_of(meta_ref[0, first + b] + w * WIN, 16)
        place = rows_ref[pl.ds(first + b, 1), :]
        one = jnp.where(iota((WIN, TOK), 0) == place - at, 1.0, 0.0).astype(BF)
        part = held[:, b * BLK : (b + 1) * BLK]
        out_ref[pl.ds(at, WIN), :] = jnp.dot(one, part, preferred_element_type=F32).astype(BF)

    enc = enc_ref[...]
    held[:HALF, :] = jnp.dot(near_ref[...], enc, preferred_element_type=F32).astype(BF)
    held[HALF:, :] = jnp.dot(far_ref[...], enc, preferred_element_type=F32).astype(BF)
    for b in range(2):
        pack(b, 0)
        for w in range(1, CAP // WIN):

            @pl.when(meta_ref[0, 2 * OWN + first + b] > w * WIN)
            def _(b=b, w=w):
                pack(b, w)


def encode_call(meta, near, far, rows, enc):
    return pl.pallas_call(
        encode_kernel,
        grid=(OWN // 2,),
        in_specs=[
            SM,
            pl.BlockSpec(near.shape, lambda i: (0, 0)),
            pl.BlockSpec(far.shape, lambda i: (0, 0)),
            pl.BlockSpec((2 * OWN, TOK), lambda i: (0, 0)),
            pl.BlockSpec((enc.shape[0], 2 * BLK), lambda i: (0, i)),
        ],
        out_specs=pl.BlockSpec((FULL, BLK), lambda i: (0, 0)),
        out_shape=jax.ShapeDtypeStruct((FULL, BLK), BF),
        scratch_shapes=[pltpu.VMEM((TOK, 2 * BLK), BF)],
        compiler_params=pltpu.CompilerParams(
            vmem_limit_bytes=32 << 20, dimension_semantics=("arbitrary",)
        ),
        cost_estimate=pl.CostEstimate(flops=6 << 30, bytes_accessed=8 << 20, transcendentals=0),
    )(meta, near, far, rows, enc)


def reduce_kernel(where_ref, meta_ref, parts_ref, bias_ref, out_ref):
    share = out_ref.shape[0]
    total = parts_ref[0].astype(F32)
    for s in range(1, parts_ref.shape[0]):
        total = total + parts_ref[s].astype(F32)
    row = iota((share, BLK), 0) + where_ref[1] * share
    bias = jnp.zeros((share, BLK), F32)
    for b in range(OWN):
        bias = jnp.where(row >= meta_ref[0, b], bias_ref[b : b + 1, :], bias)
    last = meta_ref[0, OWN - 1] + meta_ref[0, 3 * OWN - 1]
    out_ref[...] = jnp.where(row < last, jnp.maximum(total + bias, 0.0), 0.0).astype(BF)


def reduce_call(where, meta, parts, bias):
    return pl.pallas_call(
        reduce_kernel,
        in_specs=[SM, SM, VM, VM],
        out_specs=VM,
        out_shape=jax.ShapeDtypeStruct(parts.shape[1:], BF),
        compiler_params=pltpu.CompilerParams(vmem_limit_bytes=32 << 20),
        cost_estimate=pl.CostEstimate(flops=16 << 20, bytes_accessed=4 << 20, transcendentals=0),
    )(where, meta, parts, bias)


def spread_kernel(first, meta_ref, cols_ref, act_ref, out_ref):
    rows = act_ref.shape[0]

    def window(begin, place, width):
        at = pl.multiple_of(jnp.minimum(begin, rows - width), 16)
        one = jnp.where(iota((HALF, width), 1) == place - at, 1.0, 0.0).astype(BF)
        part = act_ref[pl.ds(at, width), :]
        return jnp.dot(one, part, preferred_element_type=F32).astype(BF)

    cols = cols_ref[...]
    for b in range(OWN):
        place = cols[:, first + b : first + b + 1]
        out_ref[:, b * BLK : (b + 1) * BLK] = window(meta_ref[0, first + b], place, WIN)
    for b in range(OWN):
        start, count = meta_ref[0, first + b], meta_ref[0, 2 * OWN + first + b]

        @pl.when(count > WIN)
        def _(b=b, start=start):
            begin = start + WIN
            place = cols_ref[:, first + b : first + b + 1]
            place = jnp.where(place >= begin, place, -rows)
            out_ref[:, b * BLK : (b + 1) * BLK] += window(begin, place, CAP - WIN)


def spread_call(first, meta, cols, act):
    return pl.pallas_call(
        functools.partial(spread_kernel, first),
        in_specs=[SM, VM, VM],
        out_specs=VM,
        out_shape=jax.ShapeDtypeStruct((HALF, OWN * BLK), BF),
        compiler_params=pltpu.CompilerParams(vmem_limit_bytes=32 << 20),
        cost_estimate=pl.CostEstimate(flops=1 << 30, bytes_accessed=4 << 20, transcendentals=0),
    )(meta, cols, act)


def decode_kernel(kind, half, a1_ref, a2_ref, w1_ref, w2_ref, after_ref, *outs):
    y = jnp.dot(a1_ref[...], w1_ref[...], preferred_element_type=F32)
    y = y + jnp.dot(a2_ref[...], w2_ref[...], preferred_element_type=F32)
    y = y.astype(BF)
    if kind == "x":
        outs[0][...] = y[: HALF // 2]
        outs[1][...] = y[HALF // 2 :]
        return
    z2 = []
    for zr, out in ((0, outs[0]), (1, outs[1]), (3, outs[2])):
        out[0:GRP, :] = y[zr * GRP : (zr + 1) * GRP]
        out[GRP : 2 * GRP, :] = y[HALF // 2 + zr * GRP : HALF // 2 + (zr + 1) * GRP]
    step = pl.program_id(0)
    for out, here in ((outs[3], step < half), (outs[4], step >= half)):

        @pl.when(here)
        def _(out=out):
            out[0:GRP, :] = y[2 * GRP : 3 * GRP]
            out[GRP : 2 * GRP, :] = y[HALF // 2 + 2 * GRP : HALF // 2 + 3 * GRP]


def decode_call(kind, a1, a2, w1, w2, first, width, after, tile=512):
    steps, base = width // tile, first // tile
    half = steps // 2
    depth = w1.shape[0]
    weights = pl.BlockSpec((depth, tile), lambda i: (0, base + i))
    acts = pl.BlockSpec((HALF, depth), lambda i: (0, 0))
    if kind == "x":
        shapes = [(HALF // 2, width)] * 2
        specs = [pl.BlockSpec((HALF // 2, tile), lambda i: (0, i))] * 2
    else:
        shapes = [(2 * GRP, width)] * 3 + [(2 * GRP, half * tile), (2 * GRP, width - half * tile)]
        specs = [pl.BlockSpec((2 * GRP, tile), lambda i: (0, i))] * 3 + [
            pl.BlockSpec((2 * GRP, tile), lambda i: (0, jnp.minimum(i, half - 1))),
            pl.BlockSpec((2 * GRP, tile), lambda i: (0, jnp.maximum(i - half, 0))),
        ]
    return pl.pallas_call(
        functools.partial(decode_kernel, kind, half),
        grid=(steps,),
        in_specs=[acts, acts, weights, weights, ANY],
        out_specs=specs,
        out_shape=[jax.ShapeDtypeStruct(s, BF) for s in shapes],
        compiler_params=pltpu.CompilerParams(
            vmem_limit_bytes=40 << 20, dimension_semantics=("arbitrary",)
        ),
        cost_estimate=pl.CostEstimate(
            flops=4 * HALF * depth * width,
            bytes_accessed=4 * depth * width + HALF * width * 2 + 4 * HALF * depth,
            transcendentals=0,
        ),
    )(a1, a2, w1, w2, after)


def add(*terms):
    total = terms[0].astype(F32)
    for term in terms[1:]:
        total = total + term.astype(F32)
    return total


def ring_sum(z0, z1, z3, left, right):
    h = left.shape[1]
    got_left, got_right = move(left, UP), move(right, DOWN)
    up = jnp.concatenate([add(z1[:, :h], got_left).astype(BF), z1[:, h:]], axis=1)
    down = jnp.concatenate([z3[:, :h], add(z3[:, h:], got_right).astype(BF)], axis=1)
    return add(z0, move(up, UP), move(down, DOWN))


PLAN = (("x", 2048), ("z", 2048))


def body(resid_in, active, enc_weight, enc_bias, dec_weight, target_resid, slot_block, source):
    feat_index = lax.axis_index("feat")
    section_index = lax.axis_index("section")
    sections = lax.axis_size("section")
    where = jnp.stack([feat_index, section_index]).astype(I32)
    decoder = dec_weight[0]
    other_decoder = move(decoder, SWAP_C)
    rows, cols, meta, most = index_call(where, active.T, slot_block.reshape(NPOS, 1))
    copies = jnp.broadcast_to(resid_in[None], (XL * Z,) + resid_in.shape)
    near = lax.all_to_all(copies, "feat", 0, 0, axis_index_groups=SAME_C)
    near = near.reshape(HALF, resid_in.shape[1])
    packed = encode_call(meta, near, move(near, SWAP_C), rows, enc_weight)
    bias = enc_bias.reshape(OWN, BLK)

    def exchange(room, packed):
        share = room // sections
        parts = packed[:room].reshape(sections, share, BLK)
        parts = lax.all_to_all(parts, "section", 0, 0)
        mine = reduce_call(where, meta, parts, bias)
        wide = jnp.broadcast_to(mine[None], (sections, share, BLK))
        act = lax.all_to_all(wide, "section", 0, 0).reshape(room, BLK)
        return jnp.pad(act, ((0, FULL - room), (0, 0)))

    act = lax.cond(
        most[0, 0] <= SMALL,
        functools.partial(exchange, SMALL),
        functools.partial(exchange, FULL),
        packed,
    )
    theirs = move(act, SWAP_C)
    own = spread_call(0, meta, cols, act)
    theirs = spread_call(OWN, meta, cols, theirs)

    pieces, first, after = [], 0, meta
    for kind, width in PLAN:
        outs = decode_call(kind, own, theirs, decoder, other_decoder, first, width, after)
        pieces.append((kind, width, outs))
        first, after = first + width, outs[0]
    recon = []
    for kind, width, outs in pieces:
        if kind == "x":
            stay, leave = outs
            h = width // 2
            first = move(leave[:, :h], SWAP_X)
            later, first = lax.optimization_barrier((leave[:, h:], first))
            got = jnp.concatenate([first, move(later, SWAP_X)], axis=1)
            total = add(stay, got).astype(BF).reshape(Z, GRP, width)
            recon.append(ring_sum(total[0], total[1], total[3], total[2][:, :h], total[2][:, h:]))
        else:
            total = ring_sum(*outs)
            recon.append(add(total[:GRP], move(total[GRP:].astype(BF), SWAP_X)))
    recon = jnp.concatenate(recon, axis=1)
    target = target_resid[0].astype(F32)
    keep_mask = section_index >= source[:, None]
    result = jnp.where(keep_mask, target - recon, target).astype(BF)
    return result[None]


def solution(mesh):
    placed = (
        P("feat", "section"),
        P(),
        P("section", "feat"),
        P("feat"),
        P("section", "feat", None),
        P("section", "feat", None),
        P(),
        P("feat"),
    )
    return jax.shard_map(
        body, mesh=mesh, in_specs=placed, out_specs=P("section", "feat", None), check_vma=False
    )
```

```python
import functools

import jax
import jax.numpy as jnp
from jax import lax
from jax.experimental import pallas as pl
from jax.experimental.pallas import tpu as pltpu
from jax.sharding import PartitionSpec as P

BLK = 128
GRP = 64
CAP = 384
TOK = 1024
NPOS = 256
OWN = 16
FULL = OWN * CAP
ROOMS = (2560, 3072, FULL)
WIN = 128
STEP = 8
EARLY = 768
HALF = 512
XL, Z, C = 2, 4, 2
BF = jnp.bfloat16
F32 = jnp.float32
I32 = jnp.int32
VM = pl.BlockSpec(memory_space=pltpu.VMEM)
SM = pl.BlockSpec(memory_space=pltpu.SMEM)
ANY = pl.BlockSpec(memory_space=pl.ANY)


def feat_perm(move):
    pairs = []
    for xl in range(XL):
        for z in range(Z):
            for c in range(C):
                a, b, d = move(xl, z, c)
                pairs.append(((xl * Z + z) * C + c, (a * Z + b) * C + d))
    return pairs


UP = feat_perm(lambda xl, z, c: (xl, (z + 1) % Z, c))
DOWN = feat_perm(lambda xl, z, c: (xl, (z + Z - 1) % Z, c))
SWAP_X = feat_perm(lambda xl, z, c: (1 - xl, z, c))
SWAP_C = feat_perm(lambda xl, z, c: (xl, z, 1 - c))
OTHERS = ((0, 1), (0, 3), (1, 0), (0, 2), (1, 1), (1, 3), (1, 2))


def chip(dx, dz, xl, z, c):
    return (xl + dx) % XL, (z + dz) % Z, c


def move(x, pairs):
    return lax.ppermute(x, "feat", pairs)


def iota(shape, dim):
    return lax.broadcasted_iota(I32, shape, dim)


def index_kernel(where_ref, active_ref, slot_ref, rows_ref, cols_ref, meta_ref, most_ref, hits, rowt):
    f = where_ref[0]
    xl, z, c = f // (Z * C), (f // C) % Z, f % C
    for p in range(0, NPOS, 32):
        slots = jnp.broadcast_to(slot_ref[p : p + 32, :], (32, 128))
        for t in range(0, TOK, 128):
            named = active_ref[:, t : t + 128]
            hit = named[0:1, :] == slots
            for k in range(1, active_ref.shape[0]):
                hit = jnp.logical_or(hit, named[k : k + 1, :] == slots)
            hits[p : p + 32, t : t + 128] = jnp.where(hit, 1.0, 0.0).astype(BF)
    ones = jnp.ones((TOK, 128), BF)
    every = jnp.dot(hits[...], ones, preferred_element_type=F32)
    group = jnp.where(iota((OWN, NPOS), 1) // OWN == iota((OWN, NPOS), 0), 1.0, 0.0).astype(BF)
    units = jnp.floor((every + 15.0) * (1.0 / 16.0)).astype(BF)
    totals = jnp.dot(group, units, preferred_element_type=F32) * 16.0
    most_ref[0, 0] = jnp.max(totals).astype(I32)
    other = f + 1 - 2 * c
    mine = jnp.concatenate(
        [hits[pl.ds(pl.multiple_of(o * OWN, OWN), OWN), :] for o in (f, other)], axis=0
    )
    tiles = TOK // 128
    stack = jnp.concatenate([mine[:, t * 128 : (t + 1) * 128] for t in range(tiles)], axis=0)
    i, j = iota((128, 128), 0), iota((128, 128), 1)
    inside = jnp.dot(stack, jnp.where(i < j, 1.0, 0.0).astype(BF), preferred_element_type=F32)
    sums = jnp.dot(stack, jnp.ones((128, 128), BF), preferred_element_type=F32)
    n = 2 * OWN
    running = [jnp.zeros((n, 128), F32)]
    for t in range(tiles):
        running.append(running[-1] + sums[t * n : (t + 1) * n])
    counts = running[-1]
    own_units = jnp.floor((counts + 15.0) * (1.0 / 16.0)).astype(BF)
    ci, cj = iota((n, n), 0), iota((n, n), 1)
    chain = jnp.where((cj < ci) & (ci // OWN == cj // OWN), 1.0, 0.0).astype(BF)
    starts = jnp.dot(chain, own_units, preferred_element_type=F32) * 16.0
    placed = [
        jnp.where(
            stack[t * n : (t + 1) * n].astype(F32) > 0.5,
            inside[t * n : (t + 1) * n] + running[t] + starts,
            -1.0,
        )
        for t in range(tiles)
    ]
    low = iota((n, 128), 1) < GRP
    for t in range(tiles // 2):
        even, odd = placed[2 * t], placed[2 * t + 1]
        core0 = jnp.where(low, even, pltpu.roll(odd, GRP, 1))
        core1 = jnp.where(low, pltpu.roll(even, GRP, 1), odd)
        near, far = jnp.where(c == 0, core0, core1), jnp.where(c == 0, core1, core0)
        rows_ref[:, t * 128 : (t + 1) * 128] = near.astype(I32)
        rows_ref[:, HALF + t * 128 : HALF + (t + 1) * 128] = far.astype(I32)
    blank = jnp.full((128 - n, 128), -1.0, F32)
    for t in range(tiles):
        tall = jnp.transpose(jnp.concatenate([placed[t], blank], axis=0))
        rowt[t * 128 : (t + 1) * 128, :] = tall.astype(I32)
    for xr in range(XL):
        for zr in range(Z):
            g = ((xl + xr) % XL * Z + (z + zr) % Z) * C + c
            to = (xr * Z + zr) * GRP
            cols_ref[to : to + GRP, :] = rowt[pl.ds(pl.multiple_of(g * GRP, GRP), GRP), :]
    flat = jnp.transpose(jnp.concatenate([starts, counts, jnp.zeros((64, 128), F32)], axis=0))
    meta_ref[...] = flat[0:8, :].astype(I32)


def index_call(where, active, slots):
    return pl.pallas_call(
        index_kernel,
        in_specs=[SM, VM, VM],
        out_specs=[VM, VM, VM, SM],
        out_shape=[
            jax.ShapeDtypeStruct((2 * OWN, TOK), I32),
            jax.ShapeDtypeStruct((HALF, 128), I32),
            jax.ShapeDtypeStruct((8, 128), I32),
            jax.ShapeDtypeStruct((1, 1), I32),
        ],
        scratch_shapes=[pltpu.VMEM((NPOS, TOK), BF), pltpu.VMEM((TOK, 128), I32)],
        compiler_params=pltpu.CompilerParams(vmem_limit_bytes=32 << 20),
        cost_estimate=pl.CostEstimate(flops=4 << 30, bytes_accessed=1 << 20, transcendentals=0),
    )(where, active, slots)


def gather_kernel(where_ref, *refs):
    f = where_ref[0]
    xl, z = f // (Z * C), (f // C) % Z
    for (dx, dz), ref in zip(((0, 0),) + OTHERS, refs):
        g = (xl + XL - dx) % XL * Z + (z + Z - dz) % Z
        refs[-1][pl.ds(pl.multiple_of(g * GRP, GRP), GRP), :] = ref[...]


def gather_call(where, groups, after):
    return pl.pallas_call(
        gather_kernel,
        in_specs=[SM] + [VM] * len(groups) + [ANY],
        out_specs=VM,
        out_shape=jax.ShapeDtypeStruct((HALF, groups[0].shape[1]), BF),
        compiler_params=pltpu.CompilerParams(vmem_limit_bytes=32 << 20),
        cost_estimate=pl.CostEstimate(flops=0, bytes_accessed=2 << 20, transcendentals=0),
    )(where, *groups, after)


def encode_kernel(meta_ref, half_ref, far_ref, rows_ref, enc_ref, out_ref, held):
    first = pl.program_id(0) * STEP

    def pack(b, skip, size):
        at = pl.multiple_of(meta_ref[0, first + b] + skip, 16)
        place = rows_ref[pl.ds(first + b, 1), :]
        one = jnp.where(iota((size, TOK), 0) == place - at, 1.0, 0.0).astype(BF)
        part = held[:, b * BLK : (b + 1) * BLK]
        out_ref[pl.ds(at, size), :] = jnp.dot(one, part, preferred_element_type=F32).astype(BF)

    held[:HALF, :] = half_ref[...]
    held[HALF:, :] = jnp.dot(
        far_ref[...], enc_ref[...], preferred_element_type=F32
    ).astype(BF)
    for b in range(STEP):
        pack(b, 0, WIN)

        @pl.when(meta_ref[0, 2 * OWN + first + b] > WIN)
        def _(b=b):
            pack(b, WIN, CAP - WIN)


def encode_call(meta, half, far, rows, enc):
    return pl.pallas_call(
        encode_kernel,
        grid=(OWN // STEP,),
        in_specs=[
            SM,
            pl.BlockSpec((HALF, STEP * BLK), lambda i: (0, i)),
            pl.BlockSpec(far.shape, lambda i: (0, 0)),
            pl.BlockSpec((2 * OWN, TOK), lambda i: (0, 0)),
            pl.BlockSpec((enc.shape[0], STEP * BLK), lambda i: (0, i)),
        ],
        out_specs=pl.BlockSpec((FULL, BLK), lambda i: (0, 0)),
        out_shape=jax.ShapeDtypeStruct((FULL, BLK), BF),
        scratch_shapes=[pltpu.VMEM((TOK, STEP * BLK), BF)],
        compiler_params=pltpu.CompilerParams(
            vmem_limit_bytes=32 << 20, dimension_semantics=("arbitrary",)
        ),
        cost_estimate=pl.CostEstimate(flops=4 << 30, bytes_accessed=8 << 20, transcendentals=0),
    )(meta, half, far, rows, enc)


def reduce_kernel(where_ref, meta_ref, parts_ref, bias_ref, out_ref):
    share = out_ref.shape[0]
    total = parts_ref[0].astype(F32)
    for s in range(1, parts_ref.shape[0]):
        total = total + parts_ref[s].astype(F32)
    row = iota((share, BLK), 0) + where_ref[1] * share
    bias = jnp.zeros((share, BLK), F32)
    for b in range(OWN):
        bias = jnp.where(row >= meta_ref[0, b], bias_ref[b : b + 1, :], bias)
    last = meta_ref[0, OWN - 1] + meta_ref[0, 3 * OWN - 1]
    out_ref[...] = jnp.where(row < last, jnp.maximum(total + bias, 0.0), 0.0).astype(BF)


def reduce_call(where, meta, parts, bias):
    return pl.pallas_call(
        reduce_kernel,
        in_specs=[SM, SM, VM, VM],
        out_specs=VM,
        out_shape=jax.ShapeDtypeStruct(parts.shape[1:], BF),
        compiler_params=pltpu.CompilerParams(vmem_limit_bytes=32 << 20),
        cost_estimate=pl.CostEstimate(flops=16 << 20, bytes_accessed=4 << 20, transcendentals=0),
    )(where, meta, parts, bias)


def spread_kernel(first, meta_ref, cols_ref, act_ref, out_ref):
    rows = act_ref.shape[0]

    def window(begin, place, width):
        at = pl.multiple_of(jnp.minimum(begin, rows - width), 16)
        one = jnp.where(iota((HALF, width), 1) == place - at, 1.0, 0.0).astype(BF)
        part = act_ref[pl.ds(at, width), :]
        return jnp.dot(one, part, preferred_element_type=F32).astype(BF)

    cols = cols_ref[...]
    for b in range(OWN):
        place = cols[:, first + b : first + b + 1]
        out_ref[:, b * BLK : (b + 1) * BLK] = window(meta_ref[0, first + b], place, WIN)
    for b in range(OWN):
        start, count = meta_ref[0, first + b], meta_ref[0, 2 * OWN + first + b]

        @pl.when(count > WIN)
        def _(b=b, start=start):
            begin = start + WIN
            place = cols_ref[:, first + b : first + b + 1]
            place = jnp.where(place >= begin, place, -rows)
            out_ref[:, b * BLK : (b + 1) * BLK] += window(begin, place, CAP - WIN)


def spread_call(first, meta, cols, act):
    return pl.pallas_call(
        functools.partial(spread_kernel, first),
        in_specs=[SM, VM, VM],
        out_specs=VM,
        out_shape=jax.ShapeDtypeStruct((HALF, OWN * BLK), BF),
        compiler_params=pltpu.CompilerParams(vmem_limit_bytes=32 << 20),
        cost_estimate=pl.CostEstimate(flops=1 << 30, bytes_accessed=4 << 20, transcendentals=0),
    )(meta, cols, act)


def decode_kernel(kind, half, a1_ref, a2_ref, w1_ref, w2_ref, after_ref, *outs):
    y = jnp.dot(a1_ref[...], w1_ref[...], preferred_element_type=F32)
    y = y + jnp.dot(a2_ref[...], w2_ref[...], preferred_element_type=F32)
    y = y.astype(BF)
    if kind == "x":
        outs[0][...] = y[: HALF // 2]
        outs[1][...] = y[HALF // 2 :]
        return
    z2 = []
    for zr, out in ((0, outs[0]), (1, outs[1]), (3, outs[2])):
        out[0:GRP, :] = y[zr * GRP : (zr + 1) * GRP]
        out[GRP : 2 * GRP, :] = y[HALF // 2 + zr * GRP : HALF // 2 + (zr + 1) * GRP]
    step = pl.program_id(0)
    for out, here in ((outs[3], step < half), (outs[4], step >= half)):

        @pl.when(here)
        def _(out=out):
            out[0:GRP, :] = y[2 * GRP : 3 * GRP]
            out[GRP : 2 * GRP, :] = y[HALF // 2 + 2 * GRP : HALF // 2 + 3 * GRP]


def decode_call(kind, a1, a2, w1, w2, first, width, after, tile=512):
    steps, base = width // tile, first // tile
    half = steps // 2
    depth = w1.shape[0]
    weights = pl.BlockSpec((depth, tile), lambda i: (0, base + i))
    acts = pl.BlockSpec((HALF, depth), lambda i: (0, 0))
    if kind == "x":
        shapes = [(HALF // 2, width)] * 2
        specs = [pl.BlockSpec((HALF // 2, tile), lambda i: (0, i))] * 2
    else:
        shapes = [(2 * GRP, width)] * 3 + [(2 * GRP, half * tile), (2 * GRP, width - half * tile)]
        specs = [pl.BlockSpec((2 * GRP, tile), lambda i: (0, i))] * 3 + [
            pl.BlockSpec((2 * GRP, tile), lambda i: (0, jnp.minimum(i, half - 1))),
            pl.BlockSpec((2 * GRP, tile), lambda i: (0, jnp.maximum(i - half, 0))),
        ]
    return pl.pallas_call(
        functools.partial(decode_kernel, kind, half),
        grid=(steps,),
        in_specs=[acts, acts, weights, weights, ANY],
        out_specs=specs,
        out_shape=[jax.ShapeDtypeStruct(s, BF) for s in shapes],
        compiler_params=pltpu.CompilerParams(
            vmem_limit_bytes=40 << 20, dimension_semantics=("arbitrary",)
        ),
        cost_estimate=pl.CostEstimate(
            flops=4 * HALF * depth * width,
            bytes_accessed=4 * depth * width + HALF * width * 2 + 4 * HALF * depth,
            transcendentals=0,
        ),
    )(a1, a2, w1, w2, after)


def add(*terms):
    total = terms[0].astype(F32)
    for term in terms[1:]:
        total = total + term.astype(F32)
    return total


def ring_sum(z0, z1, z3, left, right):
    h = left.shape[1]
    got_left, got_right = move(left, UP), move(right, DOWN)
    up = jnp.concatenate([add(z1[:, :h], got_left).astype(BF), z1[:, h:]], axis=1)
    down = jnp.concatenate([z3[:, :h], add(z3[:, h:], got_right).astype(BF)], axis=1)
    return add(z0, move(up, UP), move(down, DOWN))


PLAN = (("x", 2048), ("z", 2048))


def body(resid_in, active, enc_weight, enc_bias, dec_weight, target_resid, slot_block, source):
    feat_index = lax.axis_index("feat")
    section_index = lax.axis_index("section")
    sections = lax.axis_size("section")
    where = jnp.stack([feat_index, section_index]).astype(I32)
    decoder = dec_weight[0]
    rows, cols, meta, most = index_call(where, active.T, slot_block.reshape(NPOS, 1))
    near = [resid_in] + [move(resid_in, feat_perm(functools.partial(chip, *o))) for o in OTHERS]
    near = gather_call(where, near, meta)
    far = move(near, SWAP_C)
    leaving, far = lax.optimization_barrier((decoder, far))
    other_decoder = move(leaving, SWAP_C)
    half = jnp.dot(near, enc_weight, preferred_element_type=F32).astype(BF)
    packed = encode_call(meta, half, far, rows, enc_weight)
    bias = enc_bias.reshape(OWN, BLK)

    def exchange(room, packed):
        share = room // sections
        parts = packed[:room].reshape(sections, share, BLK)
        parts = lax.all_to_all(parts, "section", 0, 0)
        mine = reduce_call(where, meta, parts, bias)
        wide = jnp.broadcast_to(mine[None], (sections, share, BLK))
        act = lax.all_to_all(wide, "section", 0, 0).reshape(room, BLK)
        return jnp.pad(act, ((0, FULL - room), (0, 0)))

    act = lax.switch(
        sum((most[0, 0] > room).astype(I32) for room in ROOMS[:-1]),
        [functools.partial(exchange, room) for room in ROOMS],
        packed,
    )
    theirs = move(act, SWAP_C)
    own = spread_call(0, meta, cols, act)
    theirs = spread_call(OWN, meta, cols, theirs)

    pieces, first, after = [], 0, meta
    for kind, width in PLAN:
        outs = decode_call(kind, own, theirs, decoder, other_decoder, first, width, after)
        pieces.append((kind, width, list(outs)))
        first, after = first + width, outs[0]
    recon = []
    for kind, width, outs in pieces:
        if kind == "x":
            stay, leave = outs
            first = move(leave[:, :EARLY], SWAP_X)
            later, first, left, right = lax.optimization_barrier(
                (leave[:, EARLY:], first, pieces[1][2][3], pieces[1][2][4])
            )
            pieces[1][2][3:] = [left, right]
            got = jnp.concatenate([first, move(later, SWAP_X)], axis=1)
            total = add(stay, got).astype(BF).reshape(Z, GRP, width)
            steps = [feat_perm(functools.partial(chip, 0, k)) for k in range(1, Z)]
            recon.append(add(total[0], *[move(total[k + 1], steps[k]) for k in range(Z - 1)]))
        else:
            total = ring_sum(*outs)
            recon.append(add(total[:GRP], move(total[GRP:].astype(BF), SWAP_X)))
    recon = jnp.concatenate(recon, axis=1)
    target = target_resid[0].astype(F32)
    keep_mask = section_index >= source[:, None]
    result = jnp.where(keep_mask, target - recon, target).astype(BF)
    return result[None]


def solution(mesh):
    placed = (
        P("feat", "section"),
        P(),
        P("section", "feat"),
        P("feat"),
        P("section", "feat", None),
        P("section", "feat", None),
        P(),
        P("feat"),
    )
    return jax.shard_map(
        body, mesh=mesh, in_specs=placed, out_specs=P("section", "feat", None), check_vma=False
    )
```

```python
import functools

import jax
import jax.numpy as jnp
from jax import lax
from jax.experimental import pallas as pl
from jax.experimental.pallas import tpu as pltpu
from jax.sharding import PartitionSpec as P

BLK = 128
GRP = 64
CAP = 384
TOK = 1024
NPOS = 256
OWN = 16
FULL = OWN * CAP
ROOMS = (2560, 3072, FULL)
WIN = 128
STEP = 8
EARLY = 768
HALF = 512
XL, Z, C = 2, 4, 2
BF = jnp.bfloat16
F32 = jnp.float32
I32 = jnp.int32
VM = pl.BlockSpec(memory_space=pltpu.VMEM)
SM = pl.BlockSpec(memory_space=pltpu.SMEM)
ANY = pl.BlockSpec(memory_space=pl.ANY)


def feat_perm(move):
    pairs = []
    for xl in range(XL):
        for z in range(Z):
            for c in range(C):
                a, b, d = move(xl, z, c)
                pairs.append(((xl * Z + z) * C + c, (a * Z + b) * C + d))
    return pairs


UP = feat_perm(lambda xl, z, c: (xl, (z + 1) % Z, c))
DOWN = feat_perm(lambda xl, z, c: (xl, (z + Z - 1) % Z, c))
SWAP_X = feat_perm(lambda xl, z, c: (1 - xl, z, c))
SWAP_C = feat_perm(lambda xl, z, c: (xl, z, 1 - c))
OTHERS = ((0, 1), (0, 3), (1, 2), (0, 2), (1, 0), (1, 1), (1, 3))


def chip(dx, dz, xl, z, c):
    return (xl + dx) % XL, (z + dz) % Z, c


def move(x, pairs):
    return lax.ppermute(x, "feat", pairs)


def iota(shape, dim):
    return lax.broadcasted_iota(I32, shape, dim)


def index_kernel(where_ref, active_ref, slot_ref, rows_ref, cols_ref, meta_ref, room_ref, hits, rowt):
    f = where_ref[0]
    xl, z, c = f // (Z * C), (f // C) % Z, f % C
    slots = []
    for p in range(0, NPOS, 128):
        row = jnp.broadcast_to(slot_ref[:, p : p + 128].astype(F32), (128, 128))
        slots.append(jnp.transpose(row).astype(BF))
    slots = jnp.concatenate(slots, axis=0)
    one, zero = jnp.ones((16, 128), BF), jnp.zeros((16, 128), BF)
    for t in range(0, TOK, 128):
        named = active_ref[:, t : t + 128].astype(F32)
        named = [
            jnp.broadcast_to(named[k : k + 1, :], (16, 128)).astype(BF)
            for k in range(named.shape[0])
        ]
        for p in range(0, NPOS, 16):
            held = slots[p : p + 16, :]
            hit = zero
            for row in named:
                hit = jnp.where(row == held, one, hit)
            hits[p : p + 16, t : t + 128] = hit
    ones = jnp.ones((TOK, 128), BF)
    every = jnp.dot(hits[...], ones, preferred_element_type=F32)
    group = jnp.where(iota((OWN, NPOS), 1) // OWN == iota((OWN, NPOS), 0), 1.0, 0.0).astype(BF)
    units = jnp.floor((every + 15.0) * (1.0 / 16.0)).astype(BF)
    totals = jnp.dot(group, units, preferred_element_type=F32) * 16.0
    most = jnp.max(totals).astype(I32)
    room_ref[0, 0] = sum((most > room).astype(I32) for room in ROOMS[:-1])
    other = f + 1 - 2 * c
    mine = jnp.concatenate(
        [hits[pl.ds(pl.multiple_of(o * OWN, OWN), OWN), :] for o in (f, other)], axis=0
    )
    tiles = TOK // 128
    stack = jnp.concatenate([mine[:, t * 128 : (t + 1) * 128] for t in range(tiles)], axis=0)
    i, j = iota((128, 128), 0), iota((128, 128), 1)
    inside = jnp.dot(stack, jnp.where(i < j, 1.0, 0.0).astype(BF), preferred_element_type=F32)
    sums = jnp.dot(stack, jnp.ones((128, 128), BF), preferred_element_type=F32)
    n = 2 * OWN
    running = [jnp.zeros((n, 128), F32)]
    for t in range(tiles):
        running.append(running[-1] + sums[t * n : (t + 1) * n])
    counts = running[-1]
    own_units = jnp.floor((counts + 15.0) * (1.0 / 16.0)).astype(BF)
    ci, cj = iota((n, n), 0), iota((n, n), 1)
    chain = jnp.where((cj < ci) & (ci // OWN == cj // OWN), 1.0, 0.0).astype(BF)
    starts = jnp.dot(chain, own_units, preferred_element_type=F32) * 16.0
    placed = [
        jnp.where(
            stack[t * n : (t + 1) * n].astype(F32) > 0.5,
            inside[t * n : (t + 1) * n] + running[t] + starts,
            -1.0,
        )
        for t in range(tiles)
    ]
    low = iota((n, 128), 1) < GRP
    for t in range(tiles // 2):
        even, odd = placed[2 * t], placed[2 * t + 1]
        core0 = jnp.where(low, even, pltpu.roll(odd, GRP, 1))
        core1 = jnp.where(low, pltpu.roll(even, GRP, 1), odd)
        near, far = jnp.where(c == 0, core0, core1), jnp.where(c == 0, core1, core0)
        rows_ref[:, t * 128 : (t + 1) * 128] = near.astype(I32)
        rows_ref[:, HALF + t * 128 : HALF + (t + 1) * 128] = far.astype(I32)
    blank = jnp.full((128 - n, 128), -1.0, F32)
    for t in range(tiles):
        tall = jnp.transpose(jnp.concatenate([placed[t], blank], axis=0))
        rowt[t * 128 : (t + 1) * 128, :] = tall.astype(I32)
    for xr in range(XL):
        for zr in range(Z):
            g = ((xl + xr) % XL * Z + (z + zr) % Z) * C + c
            to = (xr * Z + zr) * GRP
            cols_ref[to : to + GRP, :] = rowt[pl.ds(pl.multiple_of(g * GRP, GRP), GRP), :]
    flat = jnp.transpose(jnp.concatenate([starts, counts, jnp.zeros((64, 128), F32)], axis=0))
    meta_ref[...] = flat[0:8, :].astype(I32)


def index_call(where, active, slots):
    return pl.pallas_call(
        index_kernel,
        in_specs=[SM, VM, VM],
        out_specs=[VM, VM, VM, SM],
        out_shape=[
            jax.ShapeDtypeStruct((2 * OWN, TOK), I32),
            jax.ShapeDtypeStruct((HALF, 128), I32),
            jax.ShapeDtypeStruct((8, 128), I32),
            jax.ShapeDtypeStruct((1, 1), I32),
        ],
        scratch_shapes=[pltpu.VMEM((NPOS, TOK), BF), pltpu.VMEM((TOK, 128), I32)],
        compiler_params=pltpu.CompilerParams(vmem_limit_bytes=32 << 20),
        cost_estimate=pl.CostEstimate(flops=4 << 30, bytes_accessed=1 << 20, transcendentals=0),
    )(where, active, slots)


def gather_kernel(where_ref, *refs):
    f = where_ref[0]
    xl, z = f // (Z * C), (f // C) % Z
    for (dx, dz), ref in zip(((0, 0),) + OTHERS, refs):
        g = (xl + XL - dx) % XL * Z + (z + Z - dz) % Z
        refs[-1][pl.ds(pl.multiple_of(g * GRP, GRP), GRP), :] = ref[...]


def gather_call(where, groups, after):
    return pl.pallas_call(
        gather_kernel,
        in_specs=[SM] + [VM] * len(groups) + [ANY],
        out_specs=VM,
        out_shape=jax.ShapeDtypeStruct((HALF, groups[0].shape[1]), BF),
        compiler_params=pltpu.CompilerParams(vmem_limit_bytes=32 << 20),
        cost_estimate=pl.CostEstimate(flops=0, bytes_accessed=2 << 20, transcendentals=0),
    )(where, *groups, after)


def encode_kernel(meta_ref, half_ref, far_ref, rows_ref, enc_ref, out_ref, held):
    first = pl.program_id(0) * STEP

    def pack(b, skip, size):
        at = pl.multiple_of(meta_ref[0, first + b] + skip, 16)
        place = rows_ref[pl.ds(first + b, 1), :]
        one = jnp.where(iota((size, TOK), 0) == place - at, 1.0, 0.0).astype(BF)
        part = held[:, b * BLK : (b + 1) * BLK]
        out_ref[pl.ds(at, size), :] = jnp.dot(one, part, preferred_element_type=F32).astype(BF)

    held[:HALF, :] = half_ref[...]
    held[HALF:, :] = jnp.dot(
        far_ref[...], enc_ref[...], preferred_element_type=F32
    ).astype(BF)
    for b in range(STEP):
        pack(b, 0, WIN)

        @pl.when(meta_ref[0, 2 * OWN + first + b] > WIN)
        def _(b=b):
            pack(b, WIN, CAP - WIN)


def encode_call(meta, half, far, rows, enc):
    return pl.pallas_call(
        encode_kernel,
        grid=(OWN // STEP,),
        in_specs=[
            SM,
            pl.BlockSpec((HALF, STEP * BLK), lambda i: (0, i)),
            pl.BlockSpec(far.shape, lambda i: (0, 0)),
            pl.BlockSpec((2 * OWN, TOK), lambda i: (0, 0)),
            pl.BlockSpec((enc.shape[0], STEP * BLK), lambda i: (0, i)),
        ],
        out_specs=pl.BlockSpec((FULL, BLK), lambda i: (0, 0)),
        out_shape=jax.ShapeDtypeStruct((FULL, BLK), BF),
        scratch_shapes=[pltpu.VMEM((TOK, STEP * BLK), BF)],
        compiler_params=pltpu.CompilerParams(
            vmem_limit_bytes=32 << 20, dimension_semantics=("arbitrary",)
        ),
        cost_estimate=pl.CostEstimate(flops=4 << 30, bytes_accessed=8 << 20, transcendentals=0),
    )(meta, half, far, rows, enc)


def reduce_kernel(where_ref, meta_ref, parts_ref, bias_ref, out_ref):
    share = out_ref.shape[0]
    total = parts_ref[0].astype(F32)
    for s in range(1, parts_ref.shape[0]):
        total = total + parts_ref[s].astype(F32)
    row = iota((share, BLK), 0) + where_ref[1] * share
    bias = jnp.zeros((share, BLK), F32)
    for b in range(OWN):
        bias = jnp.where(row >= meta_ref[0, b], bias_ref[b : b + 1, :], bias)
    last = meta_ref[0, OWN - 1] + meta_ref[0, 3 * OWN - 1]
    out_ref[...] = jnp.where(row < last, jnp.maximum(total + bias, 0.0), 0.0).astype(BF)


def reduce_call(where, meta, parts, bias):
    return pl.pallas_call(
        reduce_kernel,
        in_specs=[SM, SM, VM, VM],
        out_specs=VM,
        out_shape=jax.ShapeDtypeStruct(parts.shape[1:], BF),
        compiler_params=pltpu.CompilerParams(vmem_limit_bytes=32 << 20),
        cost_estimate=pl.CostEstimate(flops=16 << 20, bytes_accessed=4 << 20, transcendentals=0),
    )(where, meta, parts, bias)


def spread_kernel(first, meta_ref, cols_ref, act_ref, out_ref):
    rows = act_ref.shape[0]

    def window(begin, place, width):
        at = pl.multiple_of(jnp.minimum(begin, rows - width), 16)
        one = jnp.where(iota((HALF, width), 1) == place - at, 1.0, 0.0).astype(BF)
        part = act_ref[pl.ds(at, width), :]
        return jnp.dot(one, part, preferred_element_type=F32).astype(BF)

    cols = cols_ref[...]
    for b in range(OWN):
        place = cols[:, first + b : first + b + 1]
        out_ref[:, b * BLK : (b + 1) * BLK] = window(meta_ref[0, first + b], place, WIN)
    for b in range(OWN):
        start, count = meta_ref[0, first + b], meta_ref[0, 2 * OWN + first + b]

        @pl.when(count > WIN)
        def _(b=b, start=start):
            begin = start + WIN
            place = cols_ref[:, first + b : first + b + 1]
            place = jnp.where(place >= begin, place, -rows)
            out_ref[:, b * BLK : (b + 1) * BLK] += window(begin, place, CAP - WIN)


def spread_call(first, meta, cols, act):
    return pl.pallas_call(
        functools.partial(spread_kernel, first),
        in_specs=[SM, VM, VM],
        out_specs=VM,
        out_shape=jax.ShapeDtypeStruct((HALF, OWN * BLK), BF),
        compiler_params=pltpu.CompilerParams(vmem_limit_bytes=32 << 20),
        cost_estimate=pl.CostEstimate(flops=1 << 30, bytes_accessed=4 << 20, transcendentals=0),
    )(meta, cols, act)


def decode_kernel(kind, half, a1_ref, a2_ref, w1_ref, w2_ref, after_ref, *outs):
    y = jnp.dot(a1_ref[...], w1_ref[...], preferred_element_type=F32)
    y = y + jnp.dot(a2_ref[...], w2_ref[...], preferred_element_type=F32)
    y = y.astype(BF)
    if kind == "x":
        outs[0][...] = y[: HALF // 2]
        outs[1][...] = y[HALF // 2 :]
        return
    z2 = []
    for zr, out in ((0, outs[0]), (1, outs[1]), (3, outs[2])):
        out[0:GRP, :] = y[zr * GRP : (zr + 1) * GRP]
        out[GRP : 2 * GRP, :] = y[HALF // 2 + zr * GRP : HALF // 2 + (zr + 1) * GRP]
    step = pl.program_id(0)
    for out, here in ((outs[3], step < half), (outs[4], step >= half)):

        @pl.when(here)
        def _(out=out):
            out[0:GRP, :] = y[2 * GRP : 3 * GRP]
            out[GRP : 2 * GRP, :] = y[HALF // 2 + 2 * GRP : HALF // 2 + 3 * GRP]


def decode_call(kind, a1, a2, w1, w2, first, width, after, tile=512):
    steps, base = width // tile, first // tile
    half = steps // 2
    depth = w1.shape[0]
    weights = pl.BlockSpec((depth, tile), lambda i: (0, base + i))
    acts = pl.BlockSpec((HALF, depth), lambda i: (0, 0))
    if kind == "x":
        shapes = [(HALF // 2, width)] * 2
        specs = [pl.BlockSpec((HALF // 2, tile), lambda i: (0, i))] * 2
    else:
        shapes = [(2 * GRP, width)] * 3 + [(2 * GRP, half * tile), (2 * GRP, width - half * tile)]
        specs = [pl.BlockSpec((2 * GRP, tile), lambda i: (0, i))] * 3 + [
            pl.BlockSpec((2 * GRP, tile), lambda i: (0, jnp.minimum(i, half - 1))),
            pl.BlockSpec((2 * GRP, tile), lambda i: (0, jnp.maximum(i - half, 0))),
        ]
    return pl.pallas_call(
        functools.partial(decode_kernel, kind, half),
        grid=(steps,),
        in_specs=[acts, acts, weights, weights, ANY],
        out_specs=specs,
        out_shape=[jax.ShapeDtypeStruct(s, BF) for s in shapes],
        compiler_params=pltpu.CompilerParams(
            vmem_limit_bytes=40 << 20, dimension_semantics=("arbitrary",)
        ),
        cost_estimate=pl.CostEstimate(
            flops=4 * HALF * depth * width,
            bytes_accessed=4 * depth * width + HALF * width * 2 + 4 * HALF * depth,
            transcendentals=0,
        ),
    )(a1, a2, w1, w2, after)


def add(*terms):
    total = terms[0].astype(F32)
    for term in terms[1:]:
        total = total + term.astype(F32)
    return total


def ring_sum(z0, z1, z3, left, right):
    h = left.shape[1]
    got_left, got_right = move(left, UP), move(right, DOWN)
    up = jnp.concatenate([add(z1[:, :h], got_left).astype(BF), z1[:, h:]], axis=1)
    down = jnp.concatenate([z3[:, :h], add(z3[:, h:], got_right).astype(BF)], axis=1)
    return add(z0, move(up, UP), move(down, DOWN))


PLAN = (("x", 2048), ("z", 2048))


def body(resid_in, active, enc_weight, enc_bias, dec_weight, target_resid, slot_block, source):
    feat_index = lax.axis_index("feat")
    section_index = lax.axis_index("section")
    sections = lax.axis_size("section")
    where = jnp.stack([feat_index, section_index]).astype(I32)
    decoder = dec_weight[0]
    rows, cols, meta, room = index_call(where, active.T, slot_block.reshape(1, NPOS))
    near = [resid_in] + [move(resid_in, feat_perm(functools.partial(chip, *o))) for o in OTHERS]
    near = gather_call(where, near, meta)
    far = move(near, SWAP_C)
    leaving, far = lax.optimization_barrier((decoder, far))
    other_decoder = move(leaving, SWAP_C)
    half = jnp.dot(near, enc_weight, preferred_element_type=F32).astype(BF)
    packed = encode_call(meta, half, far, rows, enc_weight)
    bias = enc_bias.reshape(OWN, BLK)

    def exchange(room, packed):
        share = room // sections
        parts = packed[:room].reshape(sections, share, BLK)
        parts = lax.all_to_all(parts, "section", 0, 0)
        mine = reduce_call(where, meta, parts, bias)
        wide = jnp.broadcast_to(mine[None], (sections, share, BLK))
        act = lax.all_to_all(wide, "section", 0, 0).reshape(room, BLK)
        return jnp.pad(act, ((0, FULL - room), (0, 0)))

    act = lax.switch(
        room[0, 0],
        [functools.partial(exchange, room) for room in ROOMS],
        packed,
    )
    theirs = move(act, SWAP_C)
    own = spread_call(0, meta, cols, act)
    theirs = spread_call(OWN, meta, cols, theirs)

    pieces, first, after = [], 0, meta
    for kind, width in PLAN:
        outs = decode_call(kind, own, theirs, decoder, other_decoder, first, width, after)
        pieces.append((kind, width, list(outs)))
        first, after = first + width, outs[0]
    recon = []
    for kind, width, outs in pieces:
        if kind == "x":
            stay, leave = outs
            first = move(leave[:, :EARLY], SWAP_X)
            later, first, left, right = lax.optimization_barrier(
                (leave[:, EARLY:], first, pieces[1][2][3], pieces[1][2][4])
            )
            pieces[1][2][3:] = [left, right]
            got = jnp.concatenate([first, move(later, SWAP_X)], axis=1)
            total = add(stay, got).astype(BF).reshape(Z, GRP, width)
            steps = [feat_perm(functools.partial(chip, 0, k)) for k in range(1, Z)]
            recon.append(add(total[0], *[move(total[k + 1], steps[k]) for k in range(Z - 1)]))
        else:
            total = ring_sum(*outs)
            recon.append(add(total[:GRP], move(total[GRP:].astype(BF), SWAP_X)))
    recon = jnp.concatenate(recon, axis=1)
    target = target_resid[0].astype(F32)
    keep_mask = section_index >= source[:, None]
    result = jnp.where(keep_mask, target - recon, target).astype(BF)
    return result[None]


def solution(mesh):
    placed = (
        P("feat", "section"),
        P(),
        P("section", "feat"),
        P("feat"),
        P("section", "feat", None),
        P("section", "feat", None),
        P(),
        P("feat"),
    )
    return jax.shard_map(
        body, mesh=mesh, in_specs=placed, out_specs=P("section", "feat", None), check_vma=False
    )
```

```python
import functools

import jax
import jax.numpy as jnp
from jax import lax
from jax.experimental import pallas as pl
from jax.experimental.pallas import tpu as pltpu
from jax.sharding import PartitionSpec as P

BLK = 128
GRP = 64
CAP = 384
TOK = 1024
NPOS = 256
OWN = 16
FULL = OWN * CAP
ROOMS = (2560, 2816, 3072, FULL)
WIN = 128
STEP = 8
EARLY = 768
HALF = 512
XL, Z, C = 2, 4, 2
BF = jnp.bfloat16
F32 = jnp.float32
I32 = jnp.int32
VM = pl.BlockSpec(memory_space=pltpu.VMEM)
SM = pl.BlockSpec(memory_space=pltpu.SMEM)
ANY = pl.BlockSpec(memory_space=pl.ANY)


def feat_perm(move):
    pairs = []
    for xl in range(XL):
        for z in range(Z):
            for c in range(C):
                a, b, d = move(xl, z, c)
                pairs.append(((xl * Z + z) * C + c, (a * Z + b) * C + d))
    return pairs


UP = feat_perm(lambda xl, z, c: (xl, (z + 1) % Z, c))
DOWN = feat_perm(lambda xl, z, c: (xl, (z + Z - 1) % Z, c))
SWAP_X = feat_perm(lambda xl, z, c: (1 - xl, z, c))
SWAP_C = feat_perm(lambda xl, z, c: (xl, z, 1 - c))
OTHERS = ((0, 1), (0, 3), (1, 2), (0, 2), (1, 0), (1, 1), (1, 3))


def chip(dx, dz, xl, z, c):
    return (xl + dx) % XL, (z + dz) % Z, c


def move(x, pairs):
    return lax.ppermute(x, "feat", pairs)


def iota(shape, dim):
    return lax.broadcasted_iota(I32, shape, dim)


def index_kernel(where_ref, active_ref, slot_ref, rows_ref, cols_ref, meta_ref, room_ref, hits, rowt):
    f = where_ref[0]
    xl, z, c = f // (Z * C), (f // C) % Z, f % C
    slots = []
    for p in range(0, NPOS, 128):
        row = jnp.broadcast_to(slot_ref[:, p : p + 128].astype(F32), (128, 128))
        slots.append(jnp.transpose(row).astype(BF))
    slots = jnp.concatenate(slots, axis=0)
    one, zero = jnp.ones((16, 128), BF), jnp.zeros((16, 128), BF)
    for t in range(0, TOK, 128):
        named = active_ref[:, t : t + 128].astype(F32)
        named = [
            jnp.broadcast_to(named[k : k + 1, :], (16, 128)).astype(BF)
            for k in range(named.shape[0])
        ]
        for p in range(0, NPOS, 16):
            held = slots[p : p + 16, :]
            hit = zero
            for row in named:
                hit = jnp.where(row == held, one, hit)
            hits[p : p + 16, t : t + 128] = hit
    ones = jnp.ones((TOK, 128), BF)
    every = jnp.dot(hits[...], ones, preferred_element_type=F32)
    group = jnp.where(iota((OWN, NPOS), 1) // OWN == iota((OWN, NPOS), 0), 1.0, 0.0).astype(BF)
    units = jnp.floor((every + 15.0) * (1.0 / 16.0)).astype(BF)
    totals = jnp.dot(group, units, preferred_element_type=F32) * 16.0
    most = jnp.max(totals).astype(I32)
    room_ref[0, 0] = sum((most > room).astype(I32) for room in ROOMS[:-1])
    other = f + 1 - 2 * c
    mine = jnp.concatenate(
        [hits[pl.ds(pl.multiple_of(o * OWN, OWN), OWN), :] for o in (f, other)], axis=0
    )
    tiles = TOK // 128
    stack = jnp.concatenate([mine[:, t * 128 : (t + 1) * 128] for t in range(tiles)], axis=0)
    i, j = iota((128, 128), 0), iota((128, 128), 1)
    inside = jnp.dot(stack, jnp.where(i < j, 1.0, 0.0).astype(BF), preferred_element_type=F32)
    sums = jnp.dot(stack, jnp.ones((128, 128), BF), preferred_element_type=F32)
    n = 2 * OWN
    running = [jnp.zeros((n, 128), F32)]
    for t in range(tiles):
        running.append(running[-1] + sums[t * n : (t + 1) * n])
    counts = running[-1]
    own_units = jnp.floor((counts + 15.0) * (1.0 / 16.0)).astype(BF)
    ci, cj = iota((n, n), 0), iota((n, n), 1)
    chain = jnp.where((cj < ci) & (ci // OWN == cj // OWN), 1.0, 0.0).astype(BF)
    starts = jnp.dot(chain, own_units, preferred_element_type=F32) * 16.0
    placed = [
        jnp.where(
            stack[t * n : (t + 1) * n].astype(F32) > 0.5,
            inside[t * n : (t + 1) * n] + running[t] + starts,
            -1.0,
        )
        for t in range(tiles)
    ]
    low = iota((n, 128), 1) < GRP
    for t in range(tiles // 2):
        even, odd = placed[2 * t], placed[2 * t + 1]
        core0 = jnp.where(low, even, pltpu.roll(odd, GRP, 1))
        core1 = jnp.where(low, pltpu.roll(even, GRP, 1), odd)
        near, far = jnp.where(c == 0, core0, core1), jnp.where(c == 0, core1, core0)
        rows_ref[:, t * 128 : (t + 1) * 128] = near.astype(I32)
        rows_ref[:, HALF + t * 128 : HALF + (t + 1) * 128] = far.astype(I32)
    blank = jnp.full((128 - n, 128), -1.0, F32)
    for t in range(tiles):
        tall = jnp.transpose(jnp.concatenate([placed[t], blank], axis=0))
        rowt[t * 128 : (t + 1) * 128, :] = tall.astype(I32)
    for xr in range(XL):
        for zr in range(Z):
            g = ((xl + xr) % XL * Z + (z + zr) % Z) * C + c
            to = (xr * Z + zr) * GRP
            cols_ref[to : to + GRP, :] = rowt[pl.ds(pl.multiple_of(g * GRP, GRP), GRP), :]
    flat = jnp.transpose(jnp.concatenate([starts, counts, jnp.zeros((64, 128), F32)], axis=0))
    meta_ref[...] = flat[0:8, :].astype(I32)


def index_call(where, active, slots):
    return pl.pallas_call(
        index_kernel,
        in_specs=[SM, VM, VM],
        out_specs=[VM, VM, VM, SM],
        out_shape=[
            jax.ShapeDtypeStruct((2 * OWN, TOK), I32),
            jax.ShapeDtypeStruct((HALF, 128), I32),
            jax.ShapeDtypeStruct((8, 128), I32),
            jax.ShapeDtypeStruct((1, 1), I32),
        ],
        scratch_shapes=[pltpu.VMEM((NPOS, TOK), BF), pltpu.VMEM((TOK, 128), I32)],
        compiler_params=pltpu.CompilerParams(vmem_limit_bytes=32 << 20),
        cost_estimate=pl.CostEstimate(flops=4 << 30, bytes_accessed=1 << 20, transcendentals=0),
    )(where, active, slots)


def gather_kernel(where_ref, *refs):
    f = where_ref[0]
    xl, z = f // (Z * C), (f // C) % Z
    for (dx, dz), ref in zip(((0, 0),) + OTHERS, refs):
        g = (xl + XL - dx) % XL * Z + (z + Z - dz) % Z
        refs[-1][pl.ds(pl.multiple_of(g * GRP, GRP), GRP), :] = ref[...]


def gather_call(where, groups, after):
    return pl.pallas_call(
        gather_kernel,
        in_specs=[SM] + [VM] * len(groups) + [ANY],
        out_specs=VM,
        out_shape=jax.ShapeDtypeStruct((HALF, groups[0].shape[1]), BF),
        compiler_params=pltpu.CompilerParams(vmem_limit_bytes=32 << 20),
        cost_estimate=pl.CostEstimate(flops=0, bytes_accessed=2 << 20, transcendentals=0),
    )(where, *groups, after)


def encode_kernel(meta_ref, half_ref, far_ref, rows_ref, enc_ref, out_ref, held):
    first = pl.program_id(0) * STEP

    def pack(b, skip, size):
        at = pl.multiple_of(meta_ref[0, first + b] + skip, 16)
        place = rows_ref[pl.ds(first + b, 1), :]
        one = jnp.where(iota((size, TOK), 0) == place - at, 1.0, 0.0).astype(BF)
        part = held[:, b * BLK : (b + 1) * BLK]
        out_ref[pl.ds(at, size), :] = jnp.dot(one, part, preferred_element_type=F32).astype(BF)

    held[:HALF, :] = half_ref[...]
    held[HALF:, :] = jnp.dot(
        far_ref[...], enc_ref[...], preferred_element_type=F32
    ).astype(BF)
    for b in range(STEP):
        pack(b, 0, WIN)

        @pl.when(meta_ref[0, 2 * OWN + first + b] > WIN)
        def _(b=b):
            pack(b, WIN, CAP - WIN)


def encode_call(meta, half, far, rows, enc):
    return pl.pallas_call(
        encode_kernel,
        grid=(OWN // STEP,),
        in_specs=[
            SM,
            pl.BlockSpec((HALF, STEP * BLK), lambda i: (0, i)),
            pl.BlockSpec(far.shape, lambda i: (0, 0)),
            pl.BlockSpec((2 * OWN, TOK), lambda i: (0, 0)),
            pl.BlockSpec((enc.shape[0], STEP * BLK), lambda i: (0, i)),
        ],
        out_specs=pl.BlockSpec((FULL, BLK), lambda i: (0, 0)),
        out_shape=jax.ShapeDtypeStruct((FULL, BLK), BF),
        scratch_shapes=[pltpu.VMEM((TOK, STEP * BLK), BF)],
        compiler_params=pltpu.CompilerParams(
            vmem_limit_bytes=32 << 20, dimension_semantics=("arbitrary",)
        ),
        cost_estimate=pl.CostEstimate(flops=4 << 30, bytes_accessed=8 << 20, transcendentals=0),
    )(meta, half, far, rows, enc)


def reduce_kernel(where_ref, meta_ref, parts_ref, bias_ref, out_ref):
    share = out_ref.shape[0]
    total = parts_ref[0].astype(F32)
    for s in range(1, parts_ref.shape[0]):
        total = total + parts_ref[s].astype(F32)
    row = iota((share, BLK), 0) + where_ref[1] * share
    bias = jnp.zeros((share, BLK), F32)
    for b in range(OWN):
        bias = jnp.where(row >= meta_ref[0, b], bias_ref[b : b + 1, :], bias)
    last = meta_ref[0, OWN - 1] + meta_ref[0, 3 * OWN - 1]
    out_ref[...] = jnp.where(row < last, jnp.maximum(total + bias, 0.0), 0.0).astype(BF)


def reduce_call(where, meta, parts, bias):
    return pl.pallas_call(
        reduce_kernel,
        in_specs=[SM, SM, VM, VM],
        out_specs=VM,
        out_shape=jax.ShapeDtypeStruct(parts.shape[1:], BF),
        compiler_params=pltpu.CompilerParams(vmem_limit_bytes=32 << 20),
        cost_estimate=pl.CostEstimate(flops=16 << 20, bytes_accessed=4 << 20, transcendentals=0),
    )(where, meta, parts, bias)


def spread_kernel(first, meta_ref, cols_ref, act_ref, out_ref):
    rows = act_ref.shape[0]

    def window(begin, place, width):
        at = pl.multiple_of(jnp.minimum(begin, rows - width), 16)
        one = jnp.where(iota((HALF, width), 1) == place - at, 1.0, 0.0).astype(BF)
        part = act_ref[pl.ds(at, width), :]
        return jnp.dot(one, part, preferred_element_type=F32).astype(BF)

    cols = cols_ref[...]
    for b in range(OWN):
        place = cols[:, first + b : first + b + 1]
        out_ref[:, b * BLK : (b + 1) * BLK] = window(meta_ref[0, first + b], place, WIN)
    for b in range(OWN):
        start, count = meta_ref[0, first + b], meta_ref[0, 2 * OWN + first + b]

        @pl.when(count > WIN)
        def _(b=b, start=start):
            begin = start + WIN
            place = cols_ref[:, first + b : first + b + 1]
            place = jnp.where(place >= begin, place, -rows)
            out_ref[:, b * BLK : (b + 1) * BLK] += window(begin, place, CAP - WIN)


def spread_call(first, meta, cols, act):
    return pl.pallas_call(
        functools.partial(spread_kernel, first),
        in_specs=[SM, VM, VM],
        out_specs=VM,
        out_shape=jax.ShapeDtypeStruct((HALF, OWN * BLK), BF),
        compiler_params=pltpu.CompilerParams(vmem_limit_bytes=32 << 20),
        cost_estimate=pl.CostEstimate(flops=1 << 30, bytes_accessed=4 << 20, transcendentals=0),
    )(meta, cols, act)


def decode_kernel(kind, half, a1_ref, a2_ref, w1_ref, w2_ref, after_ref, *outs):
    y = jnp.dot(a1_ref[...], w1_ref[...], preferred_element_type=F32)
    y = y + jnp.dot(a2_ref[...], w2_ref[...], preferred_element_type=F32)
    y = y.astype(BF)
    if kind == "x":
        outs[0][...] = y[: HALF // 2]
        outs[1][...] = y[HALF // 2 :]
        return
    z2 = []
    for zr, out in ((0, outs[0]), (1, outs[1]), (3, outs[2])):
        out[0:GRP, :] = y[zr * GRP : (zr + 1) * GRP]
        out[GRP : 2 * GRP, :] = y[HALF // 2 + zr * GRP : HALF // 2 + (zr + 1) * GRP]
    step = pl.program_id(0)
    for out, here in ((outs[3], step < half), (outs[4], step >= half)):

        @pl.when(here)
        def _(out=out):
            out[0:GRP, :] = y[2 * GRP : 3 * GRP]
            out[GRP : 2 * GRP, :] = y[HALF // 2 + 2 * GRP : HALF // 2 + 3 * GRP]


def decode_call(kind, a1, a2, w1, w2, first, width, after, tile=512):
    steps, base = width // tile, first // tile
    half = steps // 2
    depth = w1.shape[0]
    weights = pl.BlockSpec((depth, tile), lambda i: (0, base + i))
    acts = pl.BlockSpec((HALF, depth), lambda i: (0, 0))
    if kind == "x":
        shapes = [(HALF // 2, width)] * 2
        specs = [pl.BlockSpec((HALF // 2, tile), lambda i: (0, i))] * 2
    else:
        shapes = [(2 * GRP, width)] * 3 + [(2 * GRP, half * tile), (2 * GRP, width - half * tile)]
        specs = [pl.BlockSpec((2 * GRP, tile), lambda i: (0, i))] * 3 + [
            pl.BlockSpec((2 * GRP, tile), lambda i: (0, jnp.minimum(i, half - 1))),
            pl.BlockSpec((2 * GRP, tile), lambda i: (0, jnp.maximum(i - half, 0))),
        ]
    return pl.pallas_call(
        functools.partial(decode_kernel, kind, half),
        grid=(steps,),
        in_specs=[acts, acts, weights, weights, ANY],
        out_specs=specs,
        out_shape=[jax.ShapeDtypeStruct(s, BF) for s in shapes],
        compiler_params=pltpu.CompilerParams(
            vmem_limit_bytes=40 << 20, dimension_semantics=("arbitrary",)
        ),
        cost_estimate=pl.CostEstimate(
            flops=4 * HALF * depth * width,
            bytes_accessed=4 * depth * width + HALF * width * 2 + 4 * HALF * depth,
            transcendentals=0,
        ),
    )(a1, a2, w1, w2, after)


def add(*terms):
    total = terms[0].astype(F32)
    for term in terms[1:]:
        total = total + term.astype(F32)
    return total


def ring_sum(z0, z1, z3, left, right):
    h = left.shape[1]
    got_left, got_right = move(left, UP), move(right, DOWN)
    up = jnp.concatenate([add(z1[:, :h], got_left).astype(BF), z1[:, h:]], axis=1)
    down = jnp.concatenate([z3[:, :h], add(z3[:, h:], got_right).astype(BF)], axis=1)
    return add(z0, move(up, UP), move(down, DOWN))


PLAN = (("x", 2048), ("z", 2048))


def body(resid_in, active, enc_weight, enc_bias, dec_weight, target_resid, slot_block, source):
    feat_index = lax.axis_index("feat")
    section_index = lax.axis_index("section")
    sections = lax.axis_size("section")
    where = jnp.stack([feat_index, section_index]).astype(I32)
    decoder = dec_weight[0]
    rows, cols, meta, room = index_call(where, active.T, slot_block.reshape(1, NPOS))
    near = [resid_in] + [move(resid_in, feat_perm(functools.partial(chip, *o))) for o in OTHERS]
    near = gather_call(where, near, meta)
    far = move(near, SWAP_C)
    half = jnp.dot(near, enc_weight, preferred_element_type=F32).astype(BF)
    leaving, half, far = lax.optimization_barrier((decoder, half, far))
    other_decoder = move(leaving, SWAP_C)
    packed = encode_call(meta, half, far, rows, enc_weight)
    bias = enc_bias.reshape(OWN, BLK)

    def exchange(room, packed):
        share = room // sections
        parts = packed[:room].reshape(sections, share, BLK)
        parts = lax.all_to_all(parts, "section", 0, 0)
        mine = reduce_call(where, meta, parts, bias)
        wide = jnp.broadcast_to(mine[None], (sections, share, BLK))
        act = lax.all_to_all(wide, "section", 0, 0).reshape(room, BLK)
        return jnp.pad(act, ((0, FULL - room), (0, 0)))

    act = lax.switch(
        room[0, 0],
        [functools.partial(exchange, room) for room in ROOMS],
        packed,
    )
    theirs = move(act, SWAP_C)
    own = spread_call(0, meta, cols, act)
    theirs = spread_call(OWN, meta, cols, theirs)

    pieces, first, after = [], 0, meta
    for kind, width in PLAN:
        outs = decode_call(kind, own, theirs, decoder, other_decoder, first, width, after)
        pieces.append((kind, width, list(outs)))
        first, after = first + width, outs[0]
    recon = []
    for kind, width, outs in pieces:
        if kind == "x":
            stay, leave = outs
            first = move(leave[:, :EARLY], SWAP_X)
            later, first, left, right = lax.optimization_barrier(
                (leave[:, EARLY:], first, pieces[1][2][3], pieces[1][2][4])
            )
            pieces[1][2][3:] = [left, right]
            got = jnp.concatenate([first, move(later, SWAP_X)], axis=1)
            total = add(stay, got).astype(BF).reshape(Z, GRP, width)
            steps = [feat_perm(functools.partial(chip, 0, k)) for k in range(1, Z)]
            recon.append(add(total[0], *[move(total[k + 1], steps[k]) for k in range(Z - 1)]))
        else:
            total = ring_sum(*outs)
            recon.append(add(total[:GRP], move(total[GRP:].astype(BF), SWAP_X)))
    recon = jnp.concatenate(recon, axis=1)
    target = target_resid[0].astype(F32)
    keep_mask = section_index >= source[:, None]
    result = jnp.where(keep_mask, target - recon, target).astype(BF)
    return result[None]


def solution(mesh):
    placed = (
        P("feat", "section"),
        P(),
        P("section", "feat"),
        P("feat"),
        P("section", "feat", None),
        P("section", "feat", None),
        P(),
        P("feat"),
    )
    return jax.shard_map(
        body, mesh=mesh, in_specs=placed, out_specs=P("section", "feat", None), check_vma=False
    )
```
